256 devices in a mesh: fsdp: 4 (over y_lo, core), ctx: 64 (over x, z, y_hi).
Axes of the slice: x: 4, y: 4 (y_hi: 2, y_lo: 2; y = y_hi * 2 + y_lo), z: 8, core: 2. Of those that a mesh axis runs over, the one named last changes fastest.
Arguments:
- hidden: bfloat16 [4, 8192, 2048], P('fsdp', 'ctx'), may hold values from -6 to 6
- queries: bfloat16 [4, 8192, 1024], P('fsdp', 'ctx'), may hold values from -6 to 6
- attn_out: bfloat16 [4, 8192, 1024], P('fsdp', 'ctx'), may hold values from -6 to 6
- grad_out: bfloat16 [4, 8192, 1024], P('fsdp', 'ctx'), may hold values from -6 to 6
- log_sums: float32 [4, 16, 8192], P('fsdp', None, 'ctx'), may hold values from 6 to 9
- block_order: int32 [4, 64], P('fsdp'), may hold values from 0 to 63, each once within a row
- w_kv: bfloat16 [2048, 512], P('fsdp'), may hold values from -0.125 to 0.125
Outputs:
- query_grads: bfloat16 [4, 8192, 1024], P('fsdp', 'ctx')
- input_grads: bfloat16 [4, 8192, 2048], P('fsdp', 'ctx')
- weight_grads: float32 [2048, 512], P(('fsdp', 'ctx'))
The draws below stay inside these ranges and needn't reach their ends.
Inputs may be any that keep to these rules, and one draw needn't show every extreme that they name: Each row of block_order is a permutation of the 64 block numbers.
All inputs are finite; a program needn't handle non-finite values.
Results may differ from the reference program's by a relative error of at most 0.013.
The reference program's roundings to bfloat16 on the way (of `key_vals`, `probs_low`, `score_grad` and `kv_grad`) count: a program that leaves them out, or rounds other values in their place, can miss the bound.
Values may be sent and summed in bfloat16 or wider, within the bound.
A program may use at most 128 MiB of HBM per device.

```python
import jax
import jax.numpy as jnp
from jax import lax

D = 2048
Q_HEADS = 16
KV_HEADS = 4
HEAD_DIM = 64
TOK_DEV = 128
SEQS = 4
LENGTH = 8192
N_CTX = 64


def steps_of(own_key, extent, shards, least, largest):
    factor_of, own = 1.0, jax.random.fold_in(own_key, 6)
    for position, shards_of in shards:
        draws = jnp.exp(jax.random.uniform(jax.random.fold_in(own, position), (shards_of,), jnp.float32, least / len(shards), largest / len(shards)))
        factor_of = factor_of * jnp.repeat(draws, extent[position] // shards_of).reshape([-1 if axis == position else 1 for axis in range(len(extent))])
    return factor_of


def normal_values(key, dims, width, reach, pieces=(), kind=jnp.bfloat16):
    entries = jax.random.normal(key, dims, jnp.float32) * width
    if len(pieces) > 0:
        entries = steps_of(key, dims, pieces, -0.22, 0.18) * entries
    return jnp.clip(entries, min=-reach, max=reach).astype(kind)


def setup_inputs(seed: int = 0) -> dict:
    key_of = jax.random.split(jax.random.key(seed), 8)
    return {
        "hidden": normal_values(key_of[0], (SEQS, LENGTH, D), 1.0, 6.0, ((0, 4), (1, 64))),
        "queries": normal_values(key_of[1], (SEQS, LENGTH, Q_HEADS * HEAD_DIM), 1.0, 6.0, ((0, 4), (1, 64))),
        "attn_out": normal_values(key_of[2], (SEQS, LENGTH, Q_HEADS * HEAD_DIM), 1.0, 6.0, ((0, 4), (1, 64))),
        "grad_out": normal_values(key_of[3], (SEQS, LENGTH, Q_HEADS * HEAD_DIM), 1.0, 6.0, ((0, 4), (1, 64))),
        "log_sums": jnp.clip(6.0 + 3.0 * jax.random.uniform(key_of[4], (SEQS, Q_HEADS, LENGTH), jnp.float32) ** steps_of(key_of[4], (SEQS, Q_HEADS, LENGTH), ((0, 4), (2, 64)), -0.2, 0.2), 6.0, 9.0),
        "block_order": jax.vmap(lambda own: jax.random.permutation(own, N_CTX))(jax.random.split(key_of[5], SEQS)).reshape((SEQS, N_CTX)).astype(jnp.int32),
        "w_kv": normal_values(key_of[6], (D, 2 * KV_HEADS * HEAD_DIM), D ** -0.5, 0.125, ((0, 4),)),
    }


def reference(hidden, queries, attn_out, grad_out, log_sums, block_order, w_kv):
    groups = Q_HEADS // KV_HEADS
    score_scale = HEAD_DIM ** -0.5
    key_width = KV_HEADS * HEAD_DIM
    query_list = []
    input_list = []
    total_weight = jnp.zeros(w_kv.shape, jnp.float32)
    for seq_index in range(SEQS):
        positions = (block_order[seq_index][:, None].astype(jnp.int32) * TOK_DEV
                     + jnp.arange(TOK_DEV, dtype=jnp.int32)[None, :]).reshape(LENGTH)
        causal_mask = positions[None, :] <= positions[:, None]
        key_vals = jnp.dot(hidden[seq_index], w_kv, preferred_element_type=jnp.float32).astype(jnp.bfloat16)
        keys_all = key_vals[:, :key_width].astype(jnp.float32).reshape(LENGTH, KV_HEADS, HEAD_DIM)
        values_all = key_vals[:, key_width:].astype(jnp.float32).reshape(LENGTH, KV_HEADS, HEAD_DIM)
        keys_head = jnp.repeat(keys_all.transpose(1, 0, 2), groups, axis=0)
        values_head = jnp.repeat(values_all.transpose(1, 0, 2), groups, axis=0)
        query_head = queries[seq_index].astype(jnp.float32).reshape(LENGTH, Q_HEADS, HEAD_DIM).transpose(1, 0, 2)
        grad_head = grad_out[seq_index].astype(jnp.float32).reshape(LENGTH, Q_HEADS, HEAD_DIM).transpose(1, 0, 2)
        output_head = attn_out[seq_index].astype(jnp.float32).reshape(LENGTH, Q_HEADS, HEAD_DIM).transpose(1, 0, 2)

        def one_head(packed):
            query, key_mat, value, grad, output, lse_row = packed
            scores = jnp.dot(query, key_mat.T) * score_scale
            probs = jnp.where(causal_mask, jnp.exp(scores - lse_row[:, None]), jnp.float32(0.0))
            probs_low = lax.optimization_barrier(probs.astype(jnp.bfloat16)).astype(jnp.float32)
            value_grad = jnp.dot(probs_low.T, grad)
            prob_grad = jnp.dot(grad, value.T)
            row_delta = jnp.sum(grad * output, axis=1)
            score_grad = lax.optimization_barrier((probs * (prob_grad - row_delta[:, None])).astype(jnp.bfloat16)).astype(jnp.float32)
            return jnp.dot(score_grad, key_mat) * score_scale, jnp.dot(score_grad.T, query) * score_scale, value_grad

        dq_head, dk_head, dv_head = lax.map(one_head, (query_head, keys_head, values_head, grad_head,
                                                       output_head, log_sums[seq_index]))
        query_list.append(dq_head.transpose(1, 0, 2).reshape(LENGTH, Q_HEADS * HEAD_DIM).astype(jnp.bfloat16))
        key_grad = dk_head.reshape(KV_HEADS, groups, LENGTH, HEAD_DIM).sum(axis=1).transpose(1, 0, 2).reshape(LENGTH, key_width)
        value_grad = dv_head.reshape(KV_HEADS, groups, LENGTH, HEAD_DIM).sum(axis=1).transpose(1, 0, 2).reshape(LENGTH, key_width)
        kv_grad = jnp.concatenate([key_grad, value_grad], axis=1).astype(jnp.bfloat16)
        input_list.append(jnp.dot(kv_grad, w_kv.T, preferred_element_type=jnp.float32).astype(jnp.bfloat16))
        total_weight = total_weight + jnp.dot(hidden[seq_index].T, kv_grad, preferred_element_type=jnp.float32)
    return jnp.stack(query_list), jnp.stack(input_list), total_weight
```

```python
import functools

import jax
import jax.numpy as jnp
from jax import lax
from jax.experimental import pallas as pl
from jax.experimental.pallas import tpu as pltpu
from jax.sharding import PartitionSpec as P

BF, F32 = jnp.bfloat16, jnp.float32
NT = (((1,), (1,)), ((), ()))
TN = (((0,), (0,)), ((), ()))
MESH = pl.DeviceIdType.MESH
Q_HEADS, KV_HEADS, HEAD_DIM = 16, 4, 64
NX, NZ = 4, 8
VMEM = pl.BlockSpec(memory_space=pltpu.VMEM)
SMEM = pl.BlockSpec(memory_space=pltpu.SMEM)


def place():
    f, c = lax.axis_index("fsdp"), lax.axis_index("ctx")
    return c // 16, (c // 2) % 8, c % 2, f // 2, f % 2


def dev(x, z, hi, lo, core):
    return {"fsdp": lo * 2 + core, "ctx": (x * 8 + z) * 2 + hi}


def rcopy(src, dst, send, recv, to):
    return pltpu.make_async_remote_copy(
        src_ref=src, dst_ref=dst, send_sem=send, recv_sem=recv, device_id=to, device_id_type=MESH
    )


def greet(to):
    pl.semaphore_signal(pltpu.get_barrier_semaphore(), inc=1, device_id=to, device_id_type=MESH)


def spread_kernel(
    hid, w, q, do, stat,
    q_buf, do_buf, stat_buf, kv_buf, w_all, hid_buf,
    kvs, acc, qs_sem, ks_sem, ws_sem, hs_sem, fs_sem, qr_sem, kr_sem, wr_sem, hr_sem, fr_sem, zs_sem, zr_sem,
):
    x, z, hi, lo, core = place()
    f = lo * 2 + core
    me = dev(x, z, hi, lo, core)
    sib = dev(x, z, hi, lo, 1 - core)
    near = dev(x, z, hi, 1 - lo, core)
    across = dev(x, z, hi, 1 - lo, 1 - core)
    far = dev(x, z, 1 - hi, 1 - lo, core)
    up, down = dev(x, (z + 1) % NZ, hi, lo, core), dev(x, (z + 7) % NZ, hi, lo, core)
    own = hi == core

    for to in (sib, near, across, far, up, down):
        greet(to)

    def greet_q(i, c):
        greet(dev((x + i // NZ) % NX, (z + i) % NZ, 1 - core, lo, hi))
        return c

    lax.fori_loop(0, 32, greet_q, 0)

    def greet_kv(i, c):
        dx, h = i // 2, i % 2

        @pl.when(jnp.logical_not((dx == 0) & own & (h == hi)))
        def _():
            greet(dev((x + dx) % NX, z, h, lo, hi))

        return c

    lax.fori_loop(0, 8, greet_kv, 0)
    pl.semaphore_wait(pltpu.get_barrier_semaphore(), 6 + 32 + 8 - own.astype(jnp.int32))

    w_own = pltpu.make_async_copy(w, w_all.at[f], ws_sem.at[3])
    w_own.start()
    half = w.shape[0] // 2
    w_sends = [
        rcopy(w.at[pl.ds(0, half)], w_all.at[f, pl.ds(0, half)], ws_sem.at[0], wr_sem.at[0], near),
        rcopy(w.at[pl.ds(half, half)], w_all.at[f, pl.ds(half, half)], ws_sem.at[1], wr_sem.at[1], far),
        rcopy(w, w_all.at[f], ws_sem.at[2], wr_sem.at[2], sib),
    ]
    for c in w_sends:
        c.start()

    slot = hi * 32 + x * 8 + z

    def q_copies(i):
        tx, tz = (x + i // NZ) % NX, (z + i) % NZ
        to = dev(tx, tz, core, lo, 1 - hi)
        rows, cols = pl.ds(pl.multiple_of(tz * 16, 16), 16), pl.ds(pl.multiple_of(tx * 256, 256), 256)
        return (
            rcopy(q.at[rows, cols], q_buf.at[slot], qs_sem.at[0], qr_sem.at[0], to),
            rcopy(do.at[rows, cols], do_buf.at[slot], qs_sem.at[1], qr_sem.at[1], to),
            rcopy(stat.at[tx, tz], stat_buf.at[slot], qs_sem.at[2], qr_sem.at[2], to),
        )

    def send_q(i, c):
        for copy in q_copies(i):
            copy.start()
        return c

    lax.fori_loop(0, 32, send_q, 0)

    def project(chunk):
        cols = pl.ds(pl.multiple_of(chunk * 512, 512), 512)
        return jnp.dot(hid[:, cols], w_all[chunk], preferred_element_type=F32)

    w_own.wait()
    acc[...] = project(f)
    w_sends[2].wait_recv()
    acc[...] += project(lo * 2 + 1 - core)
    other = (1 - lo) * 2 + core
    fwd = []
    for i in range(2):
        part = pl.ds(i * half, half)
        rcopy(w_all.at[other, part], w_all.at[other, part], ws_sem.at[i], wr_sem.at[i], near).wait_recv()
        c = rcopy(w_all.at[other, part], w_all.at[other, part], fs_sem.at[i], fr_sem.at[i], sib)
        c.start()
        fwd.append(c)
    acc[...] += project(other)
    last = (1 - lo) * 2 + 1 - core
    for i in range(2):
        part = pl.ds(i * half, half)
        rcopy(w_all.at[last, part], w_all.at[last, part], fs_sem.at[i], fr_sem.at[i], sib).wait_recv()
    key_vals = (acc[...] + project(last)).astype(BF)
    for g in range(KV_HEADS):
        kvs[g] = jnp.concatenate(
            [key_vals[:, g * 64 : g * 64 + 64], key_vals[:, 256 + g * 64 : 320 + g * 64]], axis=1
        )

    kslot = z * 8 + x * 2 + hi

    def kv_copy(dx, j):
        tx = (x + dx) % NX
        return rcopy(
            kvs.at[tx, pl.ds(j * 64, 64)], kv_buf.at[kslot], ks_sem.at[0], kr_sem.at[0], dev(tx, z, core, lo, j)
        )

    def kv_local(j):
        return pltpu.make_async_copy(kvs.at[x, pl.ds(j * 64, 64)], kv_buf.at[kslot], ks_sem.at[1])

    for dx in range(NX):
        for j in range(2):
            if dx > 0:
                kv_copy(dx, j).start()
            else:
                mine = own & (core == j)

                @pl.when(jnp.logical_not(mine))
                def _():
                    kv_copy(dx, j).start()

                @pl.when(mine)
                def _():
                    kv_local(j).start()

    def hid_copy(i, to, tf):
        cols = pl.ds(pl.multiple_of(tf * 512, 512), 512)
        return rcopy(hid.at[:, cols], hid_buf.at[f], hs_sem.at[i], hr_sem.at[i], to)

    hid_sends = [
        hid_copy(0, sib, lo * 2 + 1 - core),
        hid_copy(1, near, other),
        hid_copy(2, across, last),
    ]
    for c in hid_sends:
        c.start()
    hid_own = pltpu.make_async_copy(
        hid.at[:, pl.ds(pl.multiple_of(f * 512, 512), 512)], hid_buf.at[f], hs_sem.at[3]
    )
    hid_own.start()

    @pl.when(own)
    def _():
        pltpu.make_async_copy(kv_buf.at[0], kv_buf.at[0], ks_sem.at[1]).wait()
        rcopy(kv_buf.at[pl.ds(0, 7)], kv_buf.at[pl.ds(0, 7)], ks_sem.at[0], kr_sem.at[0], up).wait_recv()

    @pl.when(jnp.logical_not(own))
    def _():
        rcopy(kv_buf.at[pl.ds(0, 8)], kv_buf.at[pl.ds(0, 8)], ks_sem.at[0], kr_sem.at[0], up).wait_recv()

    def z_copy(d, s, src_z, to):
        part = kv_buf.at[pl.ds(pl.multiple_of(src_z * 8, 8), 8)]
        return rcopy(part, part, zs_sem.at[d, s], zr_sem.at[d, s], to)

    z_sends = []
    for s in range(4):
        if s:
            z_copy(0, s - 1, (z + 8 - s) % NZ, up).wait_recv()
        c = z_copy(0, s, (z + 8 - s) % NZ, up)
        c.start()
        z_sends.append(c)
        if s < 3:
            if s:
                z_copy(1, s - 1, (z + s) % NZ, down).wait_recv()
            c = z_copy(1, s, (z + s) % NZ, down)
            c.start()
            z_sends.append(c)

    got = pl.ds(pl.multiple_of((1 - core) * 32, 32), 32)
    theirs = pl.ds(pl.multiple_of(core * 32, 32), 32)
    bufs = (q_buf, do_buf, stat_buf)
    for i, buf in enumerate(bufs):
        rcopy(buf.at[got], buf.at[got], qs_sem.at[i], qr_sem.at[i], sib).wait_recv()
        c = rcopy(buf.at[got], buf.at[got], fs_sem.at[2 + i], fr_sem.at[2 + i], sib)
        c.start()
        fwd.append(c)
    for i, buf in enumerate(bufs):
        rcopy(buf.at[theirs], buf.at[theirs], fs_sem.at[2 + i], fr_sem.at[2 + i], sib).wait_recv()

    z_copy(0, 3, (z + 4) % NZ, up).wait_recv()
    z_copy(1, 2, (z + 3) % NZ, down).wait_recv()
    hid_own.wait()
    for i, src in enumerate((lo * 2 + 1 - core, other, last)):
        rcopy(hid_buf.at[src], hid_buf.at[src], hs_sem.at[i], hr_sem.at[i], sib).wait_recv()
    for c in hid_sends + z_sends + fwd + w_sends:
        c.wait_send()

    def done_q(i, c):
        for copy in q_copies(i):
            copy.wait_send()
        return c

    lax.fori_loop(0, 32, done_q, 0)

    for dx in range(NX):
        for j in range(2):
            if dx > 0:
                kv_copy(dx, j).wait_send()
            else:

                @pl.when(jnp.logical_not(own & (core == j)))
                def _():
                    kv_copy(dx, j).wait_send()


def spread(hid, w, q, do, stat):
    dma = pltpu.SemaphoreType.DMA
    return pl.pallas_call(
        spread_kernel,
        name="spread",
        out_shape=(
            jax.ShapeDtypeStruct((64, 16, 256), BF),
            jax.ShapeDtypeStruct((64, 16, 256), BF),
            jax.ShapeDtypeStruct((64, 1, 128), F32),
            jax.ShapeDtypeStruct((64, 64, 128), BF),
            jax.ShapeDtypeStruct((4, 512, 512), BF),
            jax.ShapeDtypeStruct((4, 128, 512), BF),
        ),
        in_specs=[VMEM] * 5,
        out_specs=[VMEM] * 6,
        scratch_shapes=[
            pltpu.VMEM((4, 128, 128), BF),
            pltpu.VMEM((128, 512), F32),
            dma((3,)), dma((2,)), dma((4,)), dma((4,)), dma((5,)),
            dma((3,)), dma((1,)), dma((3,)), dma((3,)), dma((5,)),
            dma((2, 4)), dma((2, 4)),
        ],
        compiler_params=pltpu.CompilerParams(
            collective_id=0, has_side_effects=True, vmem_limit_bytes=40 * 2**20
        ),
    )(hid, w, q, do, stat)


def attn_kernel(
    geo, order, q_ref, do_ref, stat_ref, kv_ref, dq_ref, dkv_ref,
    inv, qz, dz, kvs, kts, lse, dlt, dqt, dkv,
):
    zoff, koff = geo[0] * 16, geo[1] * 64

    def put(i, c):
        for j in range(8):
            inv[order[i * 8 + j]] = i * 8 + j
        return c

    lax.fori_loop(0, 8, put, 0)
    low = lax.broadcasted_iota(jnp.int32, (16, 128), 1) < 64
    low1 = lax.broadcasted_iota(jnp.int32, (1, 128), 1) < 64

    def q_slot(b):
        return lax.rem(b, 2) * 32 + lax.div(b, 2)

    def k_slot(b):
        c = lax.div(b, 2)
        return lax.rem(c, 8) * 8 + lax.div(c, 8) * 2 + lax.rem(b, 2)

    def sort(blk, c):
        stats = []
        for off in range(8):
            b = inv[blk * 8 + off]
            s = q_slot(b)
            for hp in range(2):
                qq = q_ref[s, :, hp * 128 : (hp + 1) * 128].astype(F32) * 0.125
                dd = do_ref[s, :, hp * 128 : (hp + 1) * 128].astype(F32)
                for ho in range(2):
                    rows = slice(off * 64 + hp * 32 + ho * 16, off * 64 + hp * 32 + ho * 16 + 16)
                    qh = qq if ho == 0 else pltpu.roll(qq, 64, 1)
                    dh = dd if ho == 1 else pltpu.roll(dd, 64, 1)
                    qz[blk, rows, :] = jnp.where(low, qh, 0.0).astype(BF)
                    dz[blk, rows, :] = jnp.where(low, 0.0, dh).astype(BF)
            kvs[blk, off * 64 : off * 64 + 64, :] = kv_ref[k_slot(b)]
            stats.append(stat_ref[s])
        for j in range(4):
            a, b = stats[2 * j], stats[2 * j + 1]
            lse[blk, :, j * 128 : (j + 1) * 128] = jnp.where(low1, a, pltpu.roll(b, 64, 1))
            dlt[blk, :, j * 128 : (j + 1) * 128] = jnp.where(low1, pltpu.roll(a, 64, 1), b)
        kts[blk] = kvs[blk].astype(F32).T[:64].astype(BF)
        dqt[blk] = jnp.zeros((64, 512), F32)
        dkv[blk] = jnp.zeros((512, 128), F32)
        return c

    lax.fori_loop(0, 8, sort, 0)

    def tile(m, c, diag):
        q, d, l, dl = qz[c], dz[c], lse[c], dlt[c]
        for a in range(2):
            keys = slice(a * 256, (a + 1) * 256)
            kv = kvs[m, keys, :]
            p = jnp.exp(lax.dot_general(kv, q, NT, preferred_element_type=F32) - l)
            if diag:
                kp = lax.broadcasted_iota(jnp.int32, (256, 512), 0) + a * 256
                qp = lax.broadcasted_iota(jnp.int32, (256, 512), 1)
                kpos = (kp // 64) * 128 + (kp % 64) + koff
                qpos = (qp // 64) * 128 + (qp % 16) + zoff
                p = jnp.where(kpos <= qpos, p, 0.0)
            dp = lax.dot_general(kv, d, NT, preferred_element_type=F32)
            ds = (p * (dp - dl)).astype(BF)
            dkv[m, keys, :] += jnp.dot(ds, q, preferred_element_type=F32) + jnp.dot(
                p.astype(BF), d, preferred_element_type=F32
            )
            dqt[c] += jnp.dot(kts[m, :, keys], ds, preferred_element_type=F32)

    def outer(m, carry):
        tile(m, m, True)

        def inner(c, carry):
            tile(m, c, False)
            return carry

        return lax.fori_loop(m + 1, 8, inner, carry)

    lax.fori_loop(0, 8, outer, 0)

    def finish(blk, c):
        for j in range(4):
            t = (dqt[blk, :, j * 128 : (j + 1) * 128] * 0.125).T
            for o in range(2):
                b = inv[blk * 8 + j * 2 + o]
                dq_ref[q_slot(b)] = jnp.concatenate(
                    [t[o * 64 + h * 16 : o * 64 + h * 16 + 16] for h in range(4)], axis=1
                )
                off = j * 2 + o
                dkv_ref[k_slot(b)] = dkv[blk, off * 64 : off * 64 + 64, :]
        return c

    lax.fori_loop(0, 8, finish, 0)


def attn(geo, order, q, do, stat, kv):
    return pl.pallas_call(
        attn_kernel,
        name="attn",
        out_shape=(jax.ShapeDtypeStruct((64, 16, 256), F32), jax.ShapeDtypeStruct((64, 64, 128), F32)),
        in_specs=[SMEM, SMEM, VMEM, VMEM, VMEM, VMEM],
        out_specs=(VMEM, VMEM),
        scratch_shapes=[
            pltpu.SMEM((64,), jnp.int32),
            pltpu.VMEM((8, 512, 128), BF),
            pltpu.VMEM((8, 512, 128), BF),
            pltpu.VMEM((8, 512, 128), BF),
            pltpu.VMEM((8, 64, 512), BF),
            pltpu.VMEM((8, 1, 512), F32),
            pltpu.VMEM((8, 1, 512), F32),
            pltpu.VMEM((8, 64, 512), F32),
            pltpu.VMEM((8, 512, 128), F32),
        ],
        compiler_params=pltpu.CompilerParams(vmem_limit_bytes=50 * 2**20),
    )(geo, order, q, do, stat, kv)


def collect_kernel(
    dq, dkv, w_all, hid_buf, dq_out, in_out, wg_out,
    dq_rx, dq_tx, rs_tx, rs_rx, fin, kvg, kvn, wpart, wx_rx, wz, wz_rx, wy, wy_rx,
    as_sem, ar_sem, qs_sem, qr_sem, zs_sem, zr_sem, ks_sem, kr_sem, fs_sem, fr_sem,
    xs_sem, xr_sem, vs_sem, vr_sem, ys_sem, yr_sem,
):
    x, z, hi, lo, core = place()
    f = lo * 2 + core
    sib = dev(x, z, hi, lo, 1 - core)
    near = dev(x, z, hi, 1 - lo, core)
    across = dev(x, z, hi, 1 - lo, 1 - core)
    pair = dev(x, z, 1 - hi, lo, core)
    up, down = dev(x, (z + 1) % NZ, hi, lo, core), dev(x, (z + 7) % NZ, hi, lo, core)
    own = hi == core

    def xdev(i):
        return dev((x + i) % NX, z, hi, lo, core)

    def zdev(i):
        return dev(x, (z + i) % NZ, hi, lo, core)

    for to in (sib, near, across, pair):
        greet(to)
    for i in range(1, NX):
        greet(xdev(i))
    for i in range(1, NZ):
        greet(zdev(i))

    def greet_q(i, c):
        greet(dev((x + i // NZ) % NX, (z + i) % NZ, core, lo, 1 - hi))
        return c

    lax.fori_loop(0, 32, greet_q, 0)

    def greet_kv(i, c):
        dx, j = i // 2, i % 2

        @pl.when(jnp.logical_not((dx == 0) & own & (j == core)))
        def _():
            greet(dev((x + dx) % NX, z, core, lo, j))

        return c

    lax.fori_loop(0, 8, greet_kv, 0)
    pl.semaphore_wait(pltpu.get_barrier_semaphore(), 4 + 3 + 7 + 32 + 8 - own.astype(jnp.int32))

    theirs = pl.ds(pl.multiple_of(core * 32, 32), 32)
    a = rcopy(dq.at[theirs], dq_rx, as_sem, ar_sem, sib)
    a.start()

    def z_send(d, s, src_z, to):
        terms = dkv[pl.ds(pl.multiple_of(src_z * 8, 8), 8)]
        if s:
            rcopy(rs_tx.at[d, s], rs_rx.at[d, s - 1], zs_sem.at[d, s - 1], zr_sem.at[d, s - 1], to).wait_recv()
            terms = terms + rs_rx[d, s - 1].astype(F32)
        rs_tx[d, s] = terms.astype(BF)
        c = rcopy(rs_tx.at[d, s], rs_rx.at[d, s], zs_sem.at[d, s], zr_sem.at[d, s], to)
        c.start()
        return c

    sends = []
    q_started = False
    for s in range(4):
        sends.append(z_send(0, s, (z + 4 - s) % NZ, up))
        if s < 3:
            sends.append(z_send(1, s, (z + 5 + s) % NZ, down))
        if s == 0:
            a.wait_recv()

            def add_q(i, c):
                for j in range(4):
                    k = i * 4 + j
                    dq_tx[k] = (dq[(1 - core) * 32 + k] + dq_rx[k]).astype(BF)
                return c

            lax.fori_loop(0, 8, add_q, 0)
            rows, cols = pl.ds(pl.multiple_of(z * 16, 16), 16), pl.ds(pl.multiple_of(x * 256, 256), 256)

            def q_copy(i):
                tx, tz = (x + i // NZ) % NX, (z + i) % NZ
                return rcopy(
                    dq_tx.at[tx * 8 + tz], dq_out.at[rows, cols], qs_sem, qr_sem, dev(tx, tz, 1 - core, lo, hi)
                )

            def send_q(i, c):
                q_copy(i).start()
                return c

            lax.fori_loop(0, 32, send_q, 0)

    rcopy(rs_tx.at[0, 3], rs_rx.at[0, 3], zs_sem.at[0, 3], zr_sem.at[0, 3], up).wait_recv()
    rcopy(rs_tx.at[1, 2], rs_rx.at[1, 2], zs_sem.at[1, 2], zr_sem.at[1, 2], down).wait_recv()
    fin[...] = (
        dkv[pl.ds(pl.multiple_of(z * 8, 8), 8)] + rs_rx[0, 3].astype(F32) + rs_rx[1, 2].astype(F32)
    ).astype(BF)

    krows = pl.ds(pl.multiple_of(core * 64, 64), 64)

    def kv_copy(dx, h):
        tx = (x + dx) % NX
        return rcopy(
            fin.at[tx * 2 + h], kvg.at[f_of(), x, krows], ks_sem.at[0], kr_sem.at[0], dev(tx, z, h, lo, hi)
        )

    def f_of():
        return lo * 2 + hi

    def kv_local(h):
        return pltpu.make_async_copy(fin.at[x * 2 + h], kvg.at[f_of(), x, krows], ks_sem.at[1])

    for dx in range(NX):
        for h in range(2):
            if dx > 0:
                kv_copy(dx, h).start()
            else:
                mine = own & (hi == h)

                @pl.when(jnp.logical_not(mine))
                def _():
                    kv_copy(dx, h).start()

                @pl.when(mine)
                def _():
                    kv_local(h).start()

    blk8 = kvg.at[0, :, pl.ds(0, 128)]

    @pl.when(own)
    def _():
        kv_local(0).wait()
        part = fin.at[pl.ds(0, 7)]
        rcopy(part, part, ks_sem.at[0], kr_sem.at[0], up).wait_recv()

    @pl.when(jnp.logical_not(own))
    def _():
        rcopy(fin, fin, ks_sem.at[0], kr_sem.at[0], up).wait_recv()

    for i, to in enumerate((sib, near, across)):
        c = rcopy(kvg.at[f], kvg.at[f], fs_sem.at[i], fr_sem.at[i], to)
        c.start()
        sends.append(c)

    def natural(i):
        kvn[i] = jnp.concatenate(
            [kvg[i, g, :, :64] for g in range(4)] + [kvg[i, g, :, 64:] for g in range(4)], axis=1
        )

    natural(f)
    for i in range(4):
        in_out[:, i * 512 : (i + 1) * 512] = lax.dot_general(
            kvn[f], w_all[i], NT, preferred_element_type=F32
        ).astype(BF)

    def grad_w(i):
        return lax.dot_general(hid_buf[i], kvn[i], TN, preferred_element_type=F32)

    wpart[...] = grad_w(f)
    for i, src in enumerate((lo * 2 + 1 - core, (1 - lo) * 2 + core, (1 - lo) * 2 + 1 - core)):
        rcopy(kvg.at[src], kvg.at[src], fs_sem.at[i], fr_sem.at[i], sib).wait_recv()
        natural(src)
        wpart[...] += grad_w(src)

    for i in range(1, NX):
        tx = (x + i) % NX
        c = rcopy(
            wpart.at[pl.ds(pl.multiple_of(tx * 128, 128), 128)], wx_rx.at[i - 1],
            xs_sem.at[i - 1], xr_sem.at[i - 1], xdev(i),
        )
        c.start()
        sends.append(c)
    total = wpart[pl.ds(pl.multiple_of(x * 128, 128), 128), :]
    for i in range(1, NX):
        rcopy(wx_rx.at[i - 1], wx_rx.at[i - 1], xs_sem.at[i - 1], xr_sem.at[i - 1], sib).wait_recv()
        total = total + wx_rx[i - 1]
    wz[...] = total
    for i in range(1, NZ):
        tz = (z + i) % NZ
        c = rcopy(
            wz.at[pl.ds(pl.multiple_of(tz * 16, 16), 16)], wz_rx.at[i - 1],
            vs_sem.at[i - 1], vr_sem.at[i - 1], zdev(i),
        )
        c.start()
        sends.append(c)
    total = wz[pl.ds(pl.multiple_of(z * 16, 16), 16), :]
    for i in range(1, NZ):
        rcopy(wz_rx.at[i - 1], wz_rx.at[i - 1], vs_sem.at[i - 1], vr_sem.at[i - 1], sib).wait_recv()
        total = total + wz_rx[i - 1]
    wy[...] = total
    c = rcopy(wy.at[pl.ds(pl.multiple_of((1 - hi) * 8, 8), 8)], wy_rx, ys_sem, yr_sem, pair)
    c.start()
    sends.append(c)
    c.wait_recv()
    wg_out[...] = wy[pl.ds(pl.multiple_of(hi * 8, 8), 8), :] + wy_rx[...]

    rcopy(dq_tx, dq_tx, qs_sem, qr_sem, sib).wait_recv()
    for c in sends + [a]:
        c.wait_send()

    def done_q(i, c):
        q_copy(i).wait_send()
        return c

    lax.fori_loop(0, 32, done_q, 0)
    for dx in range(NX):
        for h in range(2):
            if dx > 0:
                kv_copy(dx, h).wait_send()
            else:

                @pl.when(jnp.logical_not(own & (hi == h)))
                def _():
                    kv_copy(dx, h).wait_send()


def collect(dq, dkv, w_all, hid_buf):
    dma = pltpu.SemaphoreType.DMA
    return pl.pallas_call(
        collect_kernel,
        name="collect",
        out_shape=(
            jax.ShapeDtypeStruct((128, 1024), BF),
            jax.ShapeDtypeStruct((128, 2048), BF),
            jax.ShapeDtypeStruct((8, 512), F32),
        ),
        in_specs=[VMEM] * 4,
        out_specs=[VMEM] * 3,
        scratch_shapes=[
            pltpu.VMEM((32, 16, 256), F32),
            pltpu.VMEM((32, 16, 256), BF),
            pltpu.VMEM((2, 4, 8, 64, 128), BF),
            pltpu.VMEM((2, 4, 8, 64, 128), BF),
            pltpu.VMEM((8, 64, 128), BF),
            pltpu.VMEM((4, 4, 128, 128), BF),
            pltpu.VMEM((4, 128, 512), BF),
            pltpu.VMEM((512, 512), F32),
            pltpu.VMEM((3, 128, 512), F32),
            pltpu.VMEM((128, 512), F32),
            pltpu.VMEM((7, 16, 512), F32),
            pltpu.VMEM((16, 512), F32),
            pltpu.VMEM((8, 512), F32),
            dma, dma, dma, dma, dma((2, 4)), dma((2, 4)), dma((2,)), dma((1,)), dma((3,)), dma((3,)),
            dma((3,)), dma((3,)), dma((7,)), dma((7,)), dma, dma,
        ],
        compiler_params=pltpu.CompilerParams(
            collective_id=1, has_side_effects=True, vmem_limit_bytes=50 * 2**20
        ),
    )(dq, dkv, w_all, hid_buf)


def shards(hidden, queries, attn_out, grad_out, log_sums, block_order, w_kv):
    x, z, hi, lo, core = place()
    delta = jnp.sum(
        (grad_out[0].astype(F32) * attn_out[0].astype(F32)).reshape(128, Q_HEADS, HEAD_DIM), axis=2
    ).T

    def sliced(a):
        return a.reshape(4, 4, 8, 16).transpose(0, 2, 1, 3).reshape(4, 8, 64)

    stat = jnp.concatenate([sliced(log_sums[0]), sliced(delta)], axis=2).reshape(4, 8, 1, 128)
    orders = lax.all_gather(block_order[0], "fsdp", axis=0)
    order = orders[lo * 2 + hi]
    geo = jnp.stack([z, core]).astype(jnp.int32)
    q, do, st, kv, w_all, hid_buf = spread(hidden[0], w_kv, queries[0], grad_out[0], stat)
    dq, dkv = attn(geo, order, q, do, st, kv)
    dq_out, in_out, wg = collect(dq, dkv, w_all, hid_buf)
    return dq_out[None], in_out[None], wg


def solution(mesh):
    return jax.shard_map(
        shards,
        mesh=mesh,
        in_specs=(
            P("fsdp", "ctx", None),
            P("fsdp", "ctx", None),
            P("fsdp", "ctx", None),
            P("fsdp", "ctx", None),
            P("fsdp", None, "ctx"),
            P("fsdp", None),
            P("fsdp", None),
        ),
        out_specs=(P("fsdp", "ctx", None), P("fsdp", "ctx", None), P(("fsdp", "ctx"), None)),
        check_vma=False,
    )
```

```python
import functools

import jax
import jax.numpy as jnp
from jax import lax
from jax.experimental import pallas as pl
from jax.experimental.pallas import tpu as pltpu
from jax.sharding import PartitionSpec as P

BF, F32 = jnp.bfloat16, jnp.float32
NT = (((1,), (1,)), ((), ()))
TN = (((0,), (0,)), ((), ()))
MESH = pl.DeviceIdType.MESH
Q_HEADS, KV_HEADS, HEAD_DIM = 16, 4, 64
NX, NZ = 4, 8
VMEM = pl.BlockSpec(memory_space=pltpu.VMEM)


def place():
    f, c = lax.axis_index("fsdp"), lax.axis_index("ctx")
    return c // 16, (c // 2) % 8, c % 2, f // 2, f % 2


def dev(x, z, hi, lo, core):
    return {"fsdp": lo * 2 + core, "ctx": (x * 8 + z) * 2 + hi}


def rcopy(src, dst, send, recv, to):
    return pltpu.make_async_remote_copy(
        src_ref=src, dst_ref=dst, send_sem=send, recv_sem=recv, device_id=to, device_id_type=MESH
    )


def greet(to):
    pl.semaphore_signal(pltpu.get_barrier_semaphore(), inc=1, device_id=to, device_id_type=MESH)

META, W, WF, Q, QF, KV, HID, ZG, ZR, DQS, DQ, KVR, XA, CX, YR, ZW, FIN = (
    0, 1, 4, 6, 9, 12, 14, 16, 32, 48, 49, 50, 51, 55, 59, 63, 70
)
N_SEMS = 71


def backward_kernel(
    hid, w, q, do, stat, meta,
    dq_out, in_out, wg_out,
    meta_rx, order, w_all, acc, kvs, q_buf, do_buf, stat_buf, kv_buf, hid_buf,
    qz, dz, ks, kts, lse, dlt, dqt, dkv, p0, d0, p1, d1,
    dqs, dqs_tx, dqs_rx, dq_tx, rs_tx, rs_rx, finx, kvg, hid_t, wpart, c_rx, ws, y1, y1_rx, y2_rx, wz, wz_rx, wf,
    ssem, rsem,
):
    x, z, hi, lo, core = place()
    f = lo * 2 + core
    sib = dev(x, z, hi, lo, 1 - core)
    near = dev(x, z, hi, 1 - lo, core)
    far = dev(x, z, 1 - hi, 1 - lo, core)
    own = hi == core

    def xdev(i):
        return dev((x + i) % NX, z, hi, lo, core)

    def zdev(i):
        return dev(x, (z + i) % NZ, hi, lo, core)

    def copy(src, dst, sem, to):
        return rcopy(src, dst, ssem.at[sem], rsem.at[sem], to)

    def arrived(ref, sem):
        rcopy(ref, ref, ssem.at[sem], rsem.at[sem], sib).wait_recv()

    low_bit = (hi + lo) % 2
    x_end = hi * 2 + low_bit
    stays = (x == x_end) & own & (x // 2 == lo) & (x % 2 == core)

    for to in [sib, near, far, xdev(1), xdev(3)] + [zdev(i) for i in range(1, NZ)]:
        greet(to)

    def greet_q(i, c):
        greet(dev((x + i // NZ) % NX, (z + i) % NZ, 1 - core, lo, hi))
        return c

    lax.fori_loop(0, 32, greet_q, 0)

    def greet_kv(i, c):
        dx, h = i // 2, i % 2

        @pl.when(jnp.logical_not((dx == 0) & own & (h == hi)))
        def _():
            greet(dev((x + dx) % NX, z, h, lo, hi))

        return c

    lax.fori_loop(0, 8, greet_kv, 0)

    @pl.when(jnp.logical_not(stays))
    def _():
        greet(dev(f, z, x // 2, (x // 2 + x) % 2, hi))

    pl.semaphore_wait(
        pltpu.get_barrier_semaphore(), 12 + 32 + 8 + 1 - own.astype(jnp.int32) - stays.astype(jnp.int32)
    )

    w_own = pltpu.make_async_copy(w, w_all.at[f], ssem.at[N_SEMS])
    w_own.start()
    half = w.shape[0] // 2
    sends = [
        copy(w.at[pl.ds(0, half)], w_all.at[f, pl.ds(0, half)], W, near),
        copy(w.at[pl.ds(half, half)], w_all.at[f, pl.ds(half, half)], W + 1, far),
        copy(w, w_all.at[f], W + 2, sib),
        copy(meta, meta_rx, META, sib),
    ]
    for c in sends:
        c.start()

    slot = hi * 32 + x * 8 + z

    def q_copies(i):
        tx, tz = (x + i // NZ) % NX, (z + i) % NZ
        to = dev(tx, tz, core, lo, 1 - hi)
        rows, cols = pl.ds(pl.multiple_of(tz * 16, 16), 16), pl.ds(pl.multiple_of(tx * 256, 256), 256)
        return (
            copy(q.at[rows, cols], q_buf.at[slot], Q, to),
            copy(do.at[rows, cols], do_buf.at[slot], Q + 1, to),
            copy(stat.at[tx, tz], stat_buf.at[slot], Q + 2, to),
        )

    def send_q(i, c):
        for one in q_copies(i):
            one.start()
        return c

    lax.fori_loop(0, 32, send_q, 0)

    def project(chunk):
        cols = pl.ds(pl.multiple_of(chunk * 512, 512), 512)
        return jnp.dot(hid[:, cols], w_all[chunk], preferred_element_type=F32)

    w_own.wait()
    acc[...] = project(f)
    arrived(w_all.at[0], W + 2)
    acc[...] += project(lo * 2 + 1 - core)
    other, last = (1 - lo) * 2 + core, (1 - lo) * 2 + 1 - core
    for i in range(2):
        part = w_all.at[other, pl.ds(i * half, half)]
        arrived(part, W + i)
        sends.append(copy(part, part, WF + i, sib))
        sends[-1].start()
    acc[...] += project(other)
    for i in range(2):
        arrived(w_all.at[last, pl.ds(i * half, half)], WF + i)
    key_vals = (acc[...] + project(last)).astype(BF)
    for g in range(KV_HEADS):
        kvs[g] = jnp.concatenate(
            [key_vals[:, g * 64 : g * 64 + 64], key_vals[:, 256 + g * 64 : 320 + g * 64]], axis=1
        )

    def to_group(dx, j):
        tx = (x + dx) % NX
        rows, cols = pl.ds(j * 64, 64), pl.ds(pl.multiple_of(tx * 512, 512), 512)
        mine = x * 2 + hi
        return (
            (kvs.at[tx, rows], kv_buf.at[z * 8 + mine], KV + x // 2),
            (hid.at[rows, cols], hid_buf.at[mine], HID),
        ), dev(tx, z, core, lo, j)

    def to_groups(which, act):
        for dx in range(NX):
            for j in range(2):
                pieces, to = to_group(dx, j)
                if dx > 0:
                    act(copy(*pieces[which], to))
                else:
                    mine = own & (core == j)

                    @pl.when(jnp.logical_not(mine))
                    def _():
                        act(copy(*pieces[which], to))

                    @pl.when(mine)
                    def _():
                        src, dst, sem = pieces[which]
                        act(pltpu.make_async_copy(src, dst, rsem.at[sem]))

    def start(c):
        c.start()

    to_groups(0, start)
    to_groups(1, start)

    def z_part(src_z, u):
        return pl.ds(pl.multiple_of(src_z * 8 + u * 4, 4), 4)

    def z_copy(d, s, u):
        part = kv_buf.at[z_part((z + 8 - s) % NZ if d == 0 else (z + s) % NZ, u)]
        return copy(part, part, ZG + (d * 4 + s) * 2 + u, zdev(1) if d == 0 else zdev(7))

    for s in range(4):
        for u in range(2):
            if s == 0:
                arrived(kv_buf.at[pl.ds(0, 4)], KV + u)
            for d in range(2):
                if s == 3 and u != d:
                    continue
                if s:
                    z_copy(d, s - 1, u).wait_recv()
                sends.append(z_copy(d, s, u))
                sends[-1].start()

    got = pl.ds(pl.multiple_of((1 - core) * 32, 32), 32)
    theirs = pl.ds(pl.multiple_of(core * 32, 32), 32)
    bufs = (q_buf, do_buf, stat_buf)
    for i, buf in enumerate(bufs):
        arrived(buf.at[got], Q + i)
        sends.append(copy(buf.at[got], buf.at[got], QF + i, sib))
        sends[-1].start()

    arrived(meta_rx, META)

    @pl.when(own)
    def _():
        c = pltpu.make_async_copy(meta, order, ssem.at[N_SEMS])
        c.start()
        c.wait()

    @pl.when(jnp.logical_not(own))
    def _():
        c = pltpu.make_async_copy(meta_rx, order, ssem.at[N_SEMS])
        c.start()
        c.wait()

    for i, buf in enumerate(bufs):
        arrived(buf.at[theirs], QF + i)

    low = lax.broadcasted_iota(jnp.int32, (16, 128), 1) < 64
    low1 = lax.broadcasted_iota(jnp.int32, (1, 128), 1) < 64

    def sort_q(blk, c):
        stats = []
        for off in range(8):
            b = order[1, blk * 8 + off]
            s = (b % 2) * 32 + b // 2
            for hp in range(2):
                qq = q_buf[s, :, hp * 128 : (hp + 1) * 128].astype(F32) * 0.125
                dd = do_buf[s, :, hp * 128 : (hp + 1) * 128].astype(F32)
                for ho in range(2):
                    rows = slice(off * 64 + hp * 32 + ho * 16, off * 64 + hp * 32 + ho * 16 + 16)
                    qh = qq if ho == 0 else pltpu.roll(qq, 64, 1)
                    dh = dd if ho == 1 else pltpu.roll(dd, 64, 1)
                    qz[blk, rows, :] = jnp.where(low, qh, 0.0).astype(BF)
                    dz[blk, rows, :] = jnp.where(low, 0.0, dh).astype(BF)
            stats.append(stat_buf[s])
        for j in range(4):
            a, b = stats[2 * j], stats[2 * j + 1]
            lse[blk, :, j * 128 : (j + 1) * 128] = jnp.where(low1, a, pltpu.roll(b, 64, 1))
            dlt[blk, :, j * 128 : (j + 1) * 128] = jnp.where(low1, pltpu.roll(a, 64, 1), b)
        dqt[blk] = jnp.zeros((64, 512), F32)
        return c

    lax.fori_loop(0, 8, sort_q, 0)

    for d, s, u in ((0, 2, 1), (1, 2, 0), (0, 3, 0), (1, 3, 1)):
        z_copy(d, s, u).wait_recv()

    def sort_kv(blk, c):
        for off in range(8):
            b = order[1, blk * 8 + off]
            ks[blk, off * 64 : off * 64 + 64, :] = kv_buf[((b // 2) % 8) * 8 + (b // 16) * 2 + b % 2]
        kts[blk] = ks[blk].astype(F32).T[:64].astype(BF)
        return c

    lax.fori_loop(0, 8, sort_kv, 0)

    def probs(m, c, pb, db, diag):
        for a in range(2):
            keys = slice(a * 256, (a + 1) * 256)
            kv = ks[m, keys, :]
            first = a * 256 if diag else 0
            qs = slice(first, 512)
            n = 512 - first
            p = jnp.exp(lax.dot_general(kv, qz[c, qs], NT, preferred_element_type=F32) - lse[c, :, qs])
            if diag:
                kp = lax.broadcasted_iota(jnp.int32, (256, n), 0) + a * 256
                qp = lax.broadcasted_iota(jnp.int32, (256, n), 1) + first
                kpos = (kp // 64) * 128 + (kp % 64) + core * 64
                qpos = (qp // 64) * 128 + (qp % 16) + z * 16
                p = jnp.where(kpos <= qpos, p, 0.0)
            dp = lax.dot_general(kv, dz[c, qs], NT, preferred_element_type=F32)
            db[keys, qs] = (p * (dp - dlt[c, :, qs])).astype(BF)
            pb[keys, qs] = p.astype(BF)

    def dot(a, b):
        return jnp.dot(a, b, preferred_element_type=F32)

    def diag_grads(m, pb, db):
        top = dot(db[:256, :], qz[m]) + dot(pb[:256, :], dz[m])
        bottom = dot(db[256:, 256:], qz[m, 256:]) + dot(pb[256:, 256:], dz[m, 256:])
        dkv[pl.ds(m * 8, 4)] = top.reshape(4, 64, 128)
        dkv[pl.ds(m * 8 + 4, 4)] = bottom.reshape(4, 64, 128)
        dqt[m, :, :256] += dot(kts[m, :, :256], db[:256, :256])
        dqt[m, :, 256:] += dot(kts[m], db[:, 256:])

    def grads(m, c, pb, db):
        ds, p = db[...], pb[...]
        dkv[pl.ds(m * 8, 8)] += (dot(ds, qz[c]) + dot(p, dz[c])).reshape(8, 64, 128)
        dqt[c] += dot(kts[m], ds)

    def diagonal(i, c):
        probs(2 * i, 2 * i, p0, d0, True)
        probs(2 * i + 1, 2 * i + 1, p1, d1, True)
        diag_grads(2 * i, p0, d0)
        diag_grads(2 * i + 1, p1, d1)
        return c

    lax.fori_loop(0, 4, diagonal, 0)

    def following(m, c):
        wrap = c == 7
        return jnp.where(wrap, m + 1, m), jnp.where(wrap, jnp.minimum(m + 2, 7), c + 1)

    def below(i, carry):
        m, c = carry
        m1, c1 = following(m, c)
        probs(m, c, p0, d0, False)
        probs(m1, c1, p1, d1, False)
        grads(m, c, p0, d0)
        grads(m1, c1, p1, d1)
        return following(m1, c1)

    lax.fori_loop(0, 14, below, (0, 1))

    def r_copy(d, s, u):
        return copy(
            rs_tx.at[d, s, u], rs_rx.at[d, s, u], ZR + (d * 4 + s) * 2 + u, zdev(1) if d == 0 else zdev(7)
        )

    def terms(tz, u):
        parts = []
        for i in range(4):
            b = ((u * 2 + i // 2) * 8 + tz) * 2 + i % 2
            parts.append(dkv[order[0, b]][None])
        return jnp.concatenate(parts, axis=0)

    def r_step(s):
        for u in range(2):
            for d in range(2):
                if s == 0 and u != d:
                    continue
                t = terms((z + 4 - s) % NZ if d == 0 else (z + 4 + s) % NZ, u)
                if s > 1 or (s == 1 and u == d):
                    r_copy(d, s - 1, u).wait_recv()
                    t = t + rs_rx[d, s - 1, u].astype(F32)
                rs_tx[d, s, u] = t.astype(BF)
                sends.append(r_copy(d, s, u))
                sends[-1].start()

    r_step(0)

    def place_q(blk, c):
        for j in range(4):
            t = (dqt[blk, :, j * 128 : (j + 1) * 128] * 0.125).T
            for o in range(2):
                dqs[blk * 8 + j * 2 + o] = jnp.concatenate(
                    [t[o * 64 + h * 16 : o * 64 + h * 16 + 16] for h in range(4)], axis=1
                )
        return c

    lax.fori_loop(0, 8, place_q, 0)
    r_step(1)

    def give_q(i, c):
        for j in range(4):
            k = i * 4 + j
            dqs_tx[k] = dqs[order[0, k * 2 + core]]
        return c

    lax.fori_loop(0, 8, give_q, 0)
    sends.append(copy(dqs_tx, dqs_rx, DQS, sib))
    sends[-1].start()
    r_step(2)

    arrived(hid_buf, HID)
    for i in range(4):
        cols = slice(i * 128, (i + 1) * 128)
        hid_t[cols, :] = hid_buf[:, :, cols].reshape(512, 128).astype(F32).T.astype(BF)
    r_step(3)

    for u in range(2):
        t = terms(z, u)
        for d in range(2):
            r_copy(d, 3, u).wait_recv()
            t = t + rs_rx[d, 3, u].astype(F32)
        finx[x, u * 4 : u * 4 + 4] = t.astype(BF)

    def x_copy(i):
        src = (x + (0, 0, 3, 1)[i]) % NX
        part = finx.at[src] if i < 2 else finx.at[src, pl.ds((i - 2) * 4, 4)]
        return copy(part, part, XA + i, xdev((1, 3, 1, 3)[i]))

    for i in range(2):
        sends.append(x_copy(i))
        sends[-1].start()

    krows = pl.ds(pl.multiple_of(core * 64, 64), 64)

    def to_owners(act):
        for dx in range(NX):
            for h in range(2):
                tx = (x + dx) % NX
                src, dst = finx.at[x, tx * 2 + h], kvg.at[x, krows]
                if dx > 0:
                    act(copy(src, dst, KVR, dev(tx, z, h, lo, hi)))
                else:
                    mine = own & (hi == h)

                    @pl.when(jnp.logical_not(mine))
                    def _():
                        act(copy(src, dst, KVR, dev(tx, z, h, lo, hi)))

                    @pl.when(mine)
                    def _():
                        act(pltpu.make_async_copy(src, dst, rsem.at[KVR]))

    to_owners(start)

    arrived(dqs_rx, DQS)

    def add_q(i, c):
        for j in range(4):
            k = i * 4 + j
            dq_tx[k] = (dqs[order[0, k * 2 + 1 - core]] + dqs_rx[k]).astype(BF)
        return c

    lax.fori_loop(0, 8, add_q, 0)
    rows, cols = pl.ds(pl.multiple_of(z * 16, 16), 16), pl.ds(pl.multiple_of(x * 256, 256), 256)

    def q_return(i):
        tx, tz = (x + i // NZ) % NX, (z + i) % NZ
        return copy(dq_tx.at[tx * 8 + tz], dq_out.at[rows, cols], DQ, dev(tx, tz, 1 - core, lo, hi))

    def return_q(i, c):
        q_return(i).start()
        return c

    lax.fori_loop(0, 32, return_q, 0)

    def c_copy(i):
        g = (x + i) % NX
        return copy(wpart.at[1 - core, g], c_rx.at[g], CX + i, sib)

    def grad_w(i):
        g = (x + i) % NX
        r = dot(hid_t[...], finx[g].reshape(512, 128)).reshape(32, 2, 8, 128)
        for c in range(2):
            wpart[c, g] = r[:, c].reshape(256, 128)
        sends.append(c_copy(i))
        sends[-1].start()

    grad_w(0)
    for i in range(2):
        x_copy(i).wait_recv()
        sends.append(x_copy(2 + i))
        sends[-1].start()
    grad_w(3)
    grad_w(1)
    for i in range(2):
        x_copy(2 + i).wait_recv()
    grad_w(2)

    for i in (0, 3, 1, 2):
        g = (x + i) % NX
        c_copy(i).wait_recv()
        ws[g] = (wpart[core, g] + c_rx[g]).reshape(2, 2, 64, 128)

    def y_first(i):
        if i == 0:
            return copy(ws.at[pl.ds(0, 2), :, 1 - low_bit], y1_rx.at[0], YR, near)
        return copy(ws.at[pl.ds(2, 2), 1 - hi], y1_rx.at[1], YR + 1, far)

    def y_second(i):
        return copy(y1.at[i, :, 1 - (low_bit if i else hi)], y2_rx.at[i], YR + 2 + i, near if i else far)

    for i in range(2):
        sends.append(y_first(i))
        sends[-1].start()

    arrived(kvg, KVR)
    kvn = jnp.concatenate([kvg[g, :, :64] for g in range(4)] + [kvg[g, :, 64:] for g in range(4)], axis=1)
    for i in range(4):
        in_out[:, i * 512 : (i + 1) * 512] = lax.dot_general(
            kvn, w_all[i], NT, preferred_element_type=F32
        ).astype(BF)

    for i in range(2):
        y_first(i).wait_recv()
        for g in range(2):
            for k in range(2):
                kept = ws[g, k, low_bit] if i == 0 else ws[2 + g, hi, k]
                y1[i, g, k] = kept + y1_rx[i, g, k]
        sends.append(y_second(i))
        sends[-1].start()
    for i in range(2):
        y_second(i).wait_recv()
        for g in range(2):
            wz[i * 2 + g] = y1[i, g, low_bit if i else hi] + y2_rx[i, g]

    def z_rows(tz):
        return pl.ds(pl.multiple_of(tz * 8, 8), 8)

    def zw_copy(i):
        return copy(wz.at[:, z_rows((z + i) % NZ)], wz_rx.at[i - 1], ZW + i - 1, zdev(i))

    for i in range(1, NZ):
        sends.append(zw_copy(i))
        sends[-1].start()
    total = wz[:, z_rows(z)]
    for i in range(1, NZ):
        zw_copy(i).wait_recv()
        total = total + wz_rx[i - 1]
    wf[...] = jnp.concatenate([total[g, :, :64] for g in range(4)] + [total[g, :, 64:] for g in range(4)], axis=1)

    end = copy(wf, wg_out, FIN, dev(x_end, z, core, x // 2, x % 2))

    @pl.when(jnp.logical_not(stays))
    def _():
        end.start()

    @pl.when(stays)
    def _():
        pltpu.make_async_copy(wf, wg_out, rsem.at[FIN]).start()

    arrived(wg_out, FIN)
    arrived(dq_tx, DQ)
    for c in sends:
        c.wait_send()

    def done_q(i, c):
        for one in q_copies(i):
            one.wait_send()
        q_return(i).wait_send()
        return c

    lax.fori_loop(0, 32, done_q, 0)

    def sent(c):
        if c.is_remote:
            c.wait_send()

    to_groups(0, sent)
    to_groups(1, sent)
    to_owners(sent)

    @pl.when(jnp.logical_not(stays))
    def _():
        end.wait_send()


def backward(hid, w, q, do, stat, meta):
    v = pltpu.VMEM
    return pl.pallas_call(
        backward_kernel,
        name="backward",
        out_shape=(
            jax.ShapeDtypeStruct((128, 1024), BF),
            jax.ShapeDtypeStruct((128, 2048), BF),
            jax.ShapeDtypeStruct((8, 512), F32),
        ),
        in_specs=[VMEM] * 6,
        out_specs=[VMEM] * 3,
        scratch_shapes=[
            v((8, 128), jnp.int32),
            pltpu.SMEM((8, 128), jnp.int32),
            v((4, 512, 512), BF),
            v((128, 512), F32),
            v((4, 128, 128), BF),
            v((64, 16, 256), BF),
            v((64, 16, 256), BF),
            v((64, 1, 128), F32),
            v((64, 64, 128), BF),
            v((8, 64, 512), BF),
            v((8, 512, 128), BF),
            v((8, 512, 128), BF),
            v((8, 512, 128), BF),
            v((8, 64, 512), BF),
            v((8, 1, 512), F32),
            v((8, 1, 512), F32),
            v((8, 64, 512), F32),
            v((64, 64, 128), F32),
            v((512, 512), BF),
            v((512, 512), BF),
            v((512, 512), BF),
            v((512, 512), BF),
            v((64, 16, 256), F32),
            v((32, 16, 256), F32),
            v((32, 16, 256), F32),
            v((32, 16, 256), BF),
            v((2, 4, 2, 4, 64, 128), BF),
            v((2, 4, 2, 4, 64, 128), BF),
            v((4, 8, 64, 128), BF),
            v((4, 128, 128), BF),
            v((512, 512), BF),
            v((2, 4, 256, 128), F32),
            v((4, 256, 128), F32),
            v((4, 2, 2, 64, 128), F32),
            v((2, 2, 2, 64, 128), F32),
            v((2, 2, 2, 64, 128), F32),
            v((2, 2, 64, 128), F32),
            v((4, 64, 128), F32),
            v((7, 4, 8, 128), F32),
            v((8, 512), F32),
            pltpu.SemaphoreType.DMA((N_SEMS + 1,)),
            pltpu.SemaphoreType.DMA((N_SEMS,)),
        ],
        compiler_params=pltpu.CompilerParams(
            collective_id=0, has_side_effects=True, vmem_limit_bytes=56 * 2**20
        ),
    )(hid, w, q, do, stat, meta)


def shards(hidden, queries, attn_out, grad_out, log_sums, block_order, w_kv):
    delta = jnp.sum(
        (grad_out[0].astype(F32) * attn_out[0].astype(F32)).reshape(128, Q_HEADS, HEAD_DIM), axis=2
    ).T

    def sliced(a):
        return a.reshape(4, 4, 8, 16).transpose(0, 2, 1, 3).reshape(4, 8, 64)

    stat = jnp.concatenate([sliced(log_sums[0]), sliced(delta)], axis=2).reshape(4, 8, 1, 128)
    ids = lax.broadcasted_iota(jnp.int32, (64, 64), 1)
    there = block_order[0][None, :] == lax.broadcasted_iota(jnp.int32, (64, 64), 0)
    back = jnp.sum(jnp.where(there, ids, 0), axis=1)
    meta = jnp.pad(jnp.stack([block_order[0], back]), ((0, 6), (0, 64)))
    dq_out, in_out, wg = backward(hidden[0], w_kv, queries[0], grad_out[0], stat, meta)
    return dq_out[None], in_out[None], wg


def solution(mesh):
    return jax.shard_map(
        shards,
        mesh=mesh,
        in_specs=(
            P("fsdp", "ctx", None),
            P("fsdp", "ctx", None),
            P("fsdp", "ctx", None),
            P("fsdp", "ctx", None),
            P("fsdp", None, "ctx"),
            P("fsdp", None),
            P("fsdp", None),
        ),
        out_specs=(P("fsdp", "ctx", None), P("fsdp", "ctx", None), P(("fsdp", "ctx"), None)),
        check_vma=False,
    )
```

```python
import functools

import jax
import jax.numpy as jnp
from jax import lax
from jax.experimental import pallas as pl
from jax.experimental.pallas import tpu as pltpu
from jax.sharding import PartitionSpec as P

BF, F32 = jnp.bfloat16, jnp.float32
NT = (((1,), (1,)), ((), ()))
TN = (((0,), (0,)), ((), ()))
MESH = pl.DeviceIdType.MESH
Q_HEADS, KV_HEADS, HEAD_DIM = 16, 4, 64
NX, NZ = 4, 8
VMEM = pl.BlockSpec(memory_space=pltpu.VMEM)


def place():
    f, c = lax.axis_index("fsdp"), lax.axis_index("ctx")
    return c // 16, (c // 2) % 8, c % 2, f // 2, f % 2


def dev(x, z, hi, lo, core):
    return {"fsdp": lo * 2 + core, "ctx": (x * 8 + z) * 2 + hi}


def rcopy(src, dst, send, recv, to):
    return pltpu.make_async_remote_copy(
        src_ref=src, dst_ref=dst, send_sem=send, recv_sem=recv, device_id=to, device_id_type=MESH
    )


def greet(to):
    pl.semaphore_signal(pltpu.get_barrier_semaphore(), inc=1, device_id=to, device_id_type=MESH)

META, W, WF, Q, QF, KV, HID, ZG, ZR, DQS, DQ, KVR, XA, CX, WR = (
    0, 1, 4, 6, 9, 12, 16, 17, 49, 81, 82, 83, 85, 93, 97
)
N_SEMS = 98
HALF = 32


def backward_kernel(
    hid, w, q, do, stat, mine_order,
    dq_out, in_out, wg_out,
    sib_order, stored_vm, sorted_vm, stored, sorted_, w_all, acc, kvs, q_buf, do_buf, stat_buf, kv_buf0, kv_buf1, hid_buf,
    qz, dz, ks, kts, lse, dlt, dqt, dkv, pbufs, dbufs,
    dqs, dqs_tx, dqs_rx, dq_tx, d_tx, d_rx, rs_tx, rs_rx, finx, kvg, hid_t, wpart, c_rx, w_tx, w_rx,
    ssem, rsem,
):
    x, z, hi, lo, core = place()
    f = lo * 2 + core
    sib = dev(x, z, hi, lo, 1 - core)
    near = dev(x, z, hi, 1 - lo, core)
    far = dev(x, z, 1 - hi, 1 - lo, core)
    own = hi == core

    def xdev(i):
        return dev((x + i) % NX, z, hi, lo, core)

    def zdev(i):
        return dev(x, (z + i) % NZ, hi, lo, core)

    def copy(src, dst, sem, to):
        return rcopy(src, dst, ssem.at[sem], rsem.at[sem], to)

    def arrived(ref, sem):
        rcopy(ref, ref, ssem.at[sem], rsem.at[sem], sib).wait_recv()

    for to in [sib, near, far, xdev(1), xdev(3)] + [zdev(i) for i in range(1, NZ)]:
        greet(to)

    def greet_q(i, c):
        greet(dev((x + i // NZ) % NX, (z + i) % NZ, 1 - core, lo, hi))
        return c

    lax.fori_loop(0, 32, greet_q, 0)

    def greet_kv(i, c):
        dx, h = i // 2, i % 2

        @pl.when(jnp.logical_not((dx == 0) & own & (h == hi)))
        def _():
            greet(dev((x + dx) % NX, z, h, lo, hi))

        return c

    lax.fori_loop(0, 8, greet_kv, 0)

    stays = own & (x // 2 == lo) & (x % 2 == core)

    def w_from(i):
        return dev(f, (z + i) % NZ, (hi + i // 16) % 2, (lo + i // 8) % 2, hi)

    def w_to(i):
        return dev((x + i // NZ) % NX, (z + i) % NZ, core, x // 2, x % 2)

    def greet_w(i, c):
        @pl.when(jnp.logical_not(stays & (i == 0)))
        def _():
            greet(w_from(i))

        return c

    lax.fori_loop(0, 32, greet_w, 0)
    pl.semaphore_wait(
        pltpu.get_barrier_semaphore(), 12 + 32 + 8 + 32 - own.astype(jnp.int32) - stays.astype(jnp.int32)
    )

    w_own = pltpu.make_async_copy(w, w_all.at[f], ssem.at[N_SEMS])
    w_own.start()
    half = w.shape[0] // 2
    sends = [
        copy(w.at[pl.ds(0, half)], w_all.at[f, pl.ds(0, half)], W, near),
        copy(w.at[pl.ds(half, half)], w_all.at[f, pl.ds(half, half)], W + 1, far),
        copy(w, w_all.at[f], W + 2, sib),
        copy(mine_order, sib_order, META, sib),
    ]
    for c in sends:
        c.start()

    slot = hi * 32 + x * 8 + z

    def q_copies(i):
        tx, tz = (x + i // NZ) % NX, (z + i) % NZ
        to = dev(tx, tz, core, lo, 1 - hi)
        rows, cols = pl.ds(pl.multiple_of(tz * 16, 16), 16), pl.ds(pl.multiple_of(tx * 256, 256), 256)
        return (
            copy(q.at[rows, cols], q_buf.at[slot], Q, to),
            copy(do.at[rows, cols], do_buf.at[slot], Q + 1, to),
            copy(stat.at[tx, tz], stat_buf.at[slot], Q + 2, to),
        )

    def send_q(i, c):
        for one in q_copies(i):
            one.start()
        return c

    lax.fori_loop(0, 32, send_q, 0)

    def project(chunk):
        cols = pl.ds(pl.multiple_of(chunk * 512, 512), 512)
        return jnp.dot(hid[:, cols], w_all[chunk], preferred_element_type=F32)

    w_own.wait()
    acc[...] = project(f)
    arrived(w_all.at[0], W + 2)
    acc[...] += project(lo * 2 + 1 - core)
    other, last = (1 - lo) * 2 + core, (1 - lo) * 2 + 1 - core
    for i in range(2):
        part = w_all.at[other, pl.ds(i * half, half)]
        arrived(part, W + i)
        sends.append(copy(part, part, WF + i, sib))
        sends[-1].start()
    acc[...] += project(other)
    for i in range(2):
        arrived(w_all.at[last, pl.ds(i * half, half)], WF + i)
    key_vals = (acc[...] + project(last)).astype(BF)
    for g in range(KV_HEADS):
        kvs[g] = jnp.concatenate(
            [key_vals[:, g * 64 : g * 64 + 64], key_vals[:, 256 + g * 64 : 320 + g * 64]], axis=1
        )

    kv_buf = (kv_buf0, kv_buf1)

    def to_group(dx, j, which):
        tx = (x + dx) % NX
        to = dev(tx, z, core, lo, j)
        mine = x * 2 + hi
        if which < 2:
            rows = pl.ds(j * 64 + which * HALF, HALF)
            return (kvs.at[tx, rows], kv_buf[which].at[z * 8 + mine], KV + which * 2 + x // 2), to
        rows, cols = pl.ds(j * 64, 64), pl.ds(pl.multiple_of(tx * 512, 512), 512)
        return (hid.at[rows, cols], hid_buf.at[mine], HID), to

    def to_groups(which, act):
        for dx in range(NX):
            for j in range(2):
                piece, to = to_group(dx, j, which)
                if dx > 0:
                    act(copy(*piece, to))
                else:
                    mine = own & (core == j)

                    @pl.when(jnp.logical_not(mine))
                    def _():
                        act(copy(*piece, to))

                    @pl.when(mine)
                    def _():
                        src, dst, sem = piece
                        act(pltpu.make_async_copy(src, dst, rsem.at[sem]))

    def start(c):
        c.start()

    to_groups(0, start)
    to_groups(1, start)

    def z_part(src_z, u):
        return pl.ds(pl.multiple_of(src_z * 8 + u * 4, 4), 4)

    def z_copy(e, d, s, u):
        part = kv_buf[e].at[z_part((z + 8 - s) % NZ if d == 0 else (z + s) % NZ, u)]
        return copy(part, part, ZG + e * 16 + (d * 4 + s) * 2 + u, zdev(1) if d == 0 else zdev(7))

    def z_step(e, s):
        for u in range(2):
            if s == 0:
                arrived(kv_buf[e].at[pl.ds(0, 4)], KV + e * 2 + u)
            for d in range(2):
                if s == 3 and u != d:
                    continue
                if s:
                    z_copy(e, d, s - 1, u).wait_recv()
                sends.append(z_copy(e, d, s, u))
                sends[-1].start()

    def z_end(e):
        for d, s, u in ((0, 2, 1), (1, 2, 0), (0, 3, 0), (1, 3, 1)):
            z_copy(e, d, s, u).wait_recv()

    z_step(0, 0)
    z_step(0, 1)
    z_step(1, 0)
    z_step(0, 2)
    z_step(0, 3)
    z_step(1, 1)

    got = pl.ds(pl.multiple_of((1 - core) * 32, 32), 32)
    theirs = pl.ds(pl.multiple_of(core * 32, 32), 32)
    bufs = (q_buf, do_buf, stat_buf)
    for i, buf in enumerate(bufs):
        arrived(buf.at[got], Q + i)
        sends.append(copy(buf.at[got], buf.at[got], QF + i, sib))
        sends[-1].start()

    arrived(sib_order, META)
    there = jnp.where(own, mine_order[...], sib_order[...])
    ids = lax.broadcasted_iota(jnp.int32, (64, 64), 1)
    back = jnp.max(jnp.where(there == lax.broadcasted_iota(jnp.int32, (64, 64), 0), ids, 0), axis=1, keepdims=True)
    stored_vm[...] = there
    sorted_vm[...] = jnp.broadcast_to(back, (64, 128))
    for vm, sm in ((stored_vm, stored), (sorted_vm, sorted_)):
        c = pltpu.make_async_copy(vm, sm, ssem.at[N_SEMS])
        c.start()
        c.wait()

    for i, buf in enumerate(bufs):
        arrived(buf.at[theirs], QF + i)

    low = lax.broadcasted_iota(jnp.int32, (16, 128), 1) < 64
    low1 = lax.broadcasted_iota(jnp.int32, (1, 128), 1) < 64

    def sort_q(blk, c):
        stats = []
        for off in range(8):
            b = sorted_[blk * 8 + off, 0]
            s = (b % 2) * 32 + b // 2
            for hp in range(2):
                qq = q_buf[s, :, hp * 128 : (hp + 1) * 128].astype(F32) * 0.125
                dd = do_buf[s, :, hp * 128 : (hp + 1) * 128].astype(F32)
                for ho in range(2):
                    rows = slice(off * 64 + hp * 32 + ho * 16, off * 64 + hp * 32 + ho * 16 + 16)
                    qh = qq if ho == 0 else pltpu.roll(qq, 64, 1)
                    dh = dd if ho == 1 else pltpu.roll(dd, 64, 1)
                    qz[blk, rows, :] = jnp.where(low, qh, 0.0).astype(BF)
                    dz[blk, rows, :] = jnp.where(low, 0.0, dh).astype(BF)
            stats.append(stat_buf[s])
        for j in range(4):
            a, b = stats[2 * j], stats[2 * j + 1]
            lse[blk, :, j * 128 : (j + 1) * 128] = jnp.where(low1, a, pltpu.roll(b, 64, 1))
            dlt[blk, :, j * 128 : (j + 1) * 128] = jnp.where(low1, pltpu.roll(a, 64, 1), b)
        dqt[blk] = jnp.zeros((64, 512), F32)
        return c

    lax.fori_loop(0, 8, sort_q, 0)

    def sort_kv(e):
        def one(blk, c):
            for off in range(8):
                b = sorted_[blk * 8 + off, 0]
                ks[blk, off * HALF : (off + 1) * HALF, :] = kv_buf[e][((b // 2) % 8) * 8 + (b // 16) * 2 + b % 2]
            kts[blk] = ks[blk].astype(F32).T[:64].astype(BF)
            return c

        lax.fori_loop(0, 8, one, 0)

    def probs(m, c, t, e=None):
        for n, qs in ((256, slice(0, 512)),) if e is None else ((128, slice(0, 256)), (256, slice(256, 512))):
            keys = slice(0, n)
            kv = ks[m, keys, :]
            p = jnp.exp(lax.dot_general(kv, qz[c, qs], NT, preferred_element_type=F32) - lse[c, :, qs])
            if e is not None:
                kp = lax.broadcasted_iota(jnp.int32, p.shape, 0)
                qp = lax.broadcasted_iota(jnp.int32, p.shape, 1) + qs.start
                kpos = (kp // HALF) * 128 + (kp % HALF) + core * 64 + e * HALF
                qpos = (qp // 64) * 128 + (qp % 16) + z * 16
                p = jnp.where(kpos <= qpos, p, 0.0)
            dp = lax.dot_general(kv, dz[c, qs], NT, preferred_element_type=F32)
            dbufs[t, keys, qs] = (p * (dp - dlt[c, :, qs])).astype(BF)
            pbufs[t, keys, qs] = p.astype(BF)

    def dot(a, b):
        return jnp.dot(a, b, preferred_element_type=F32)

    def diag_grads(e, m, t):
        top = dot(dbufs[t, :128, :], qz[m]) + dot(pbufs[t, :128, :], dz[m])
        bottom = dot(dbufs[t, 128:, 256:], qz[m, 256:]) + dot(pbufs[t, 128:, 256:], dz[m, 256:])
        dkv[e, pl.ds(m * 8, 4)] = top.reshape(4, HALF, 128)
        dkv[e, pl.ds(m * 8 + 4, 4)] = bottom.reshape(4, HALF, 128)
        dqt[m, :, :256] += dot(kts[m, :, :128], dbufs[t, :128, :256])
        dqt[m, :, 256:] += dot(kts[m], dbufs[t, :, 256:])

    def grads(e, m, c, t):
        ds, p = dbufs[t], pbufs[t]
        dkv[e, pl.ds(m * 8, 8)] += (dot(ds, qz[c]) + dot(p, dz[c])).reshape(8, HALF, 128)
        dqt[c] += dot(kts[m], ds)

    def diagonal(e):
        def one(i, c):
            for t in range(4):
                probs(4 * i + t, 4 * i + t, t, e)
            for t in range(4):
                diag_grads(e, 4 * i + t, t)
            return c

        lax.fori_loop(0, 2, one, 0)

    def following(m, c):
        wrap = c == 7
        return jnp.where(wrap, m + 1, m), jnp.where(wrap, jnp.minimum(m + 2, 7), c + 1)

    def below(e, n, at):
        def four(i, at):
            tiles = [at]
            for t in range(4):
                probs(*tiles[t], t)
                tiles.append(following(*tiles[t]))
            for t in range(4):
                grads(e, *tiles[t], t)
            return tiles[4]

        return lax.fori_loop(0, n, four, at)

    def r_copy(d, s, u):
        return copy(
            rs_tx.at[d, s, u], rs_rx.at[d, s, u], ZR + 16 + (d * 4 + s) * 2 + u, zdev(1) if d == 0 else zdev(7)
        )

    def terms(e, tz, u):
        parts = []
        for i in range(4):
            b = ((u * 2 + i // 2) * 8 + tz) * 2 + i % 2
            parts.append(dkv[e, stored[0, b]][None])
        return jnp.concatenate(parts, axis=0)

    def r_step(s):
        for u in range(2):
            for d in range(2):
                if s == 0 and u != d:
                    continue
                t = terms(1, (z + 4 - s) % NZ if d == 0 else (z + 4 + s) % NZ, u)
                if s > 1 or (s == 1 and u == d):
                    r_copy(d, s - 1, u).wait_recv()
                    t = t + rs_rx[d, s - 1, u].astype(F32)
                rs_tx[d, s, u] = t.astype(BF)
                sends.append(r_copy(d, s, u))
                sends[-1].start()

    def d_copy(i):
        return copy(d_tx.at[i - 1], d_rx.at[i - 1], ZR + i, zdev(i))

    def d_send():
        for i in (4, 3, 5, 2, 6, 1, 7):
            for u in range(2):
                d_tx[i - 1, u * 4 : u * 4 + 4] = terms(0, (z + i) % NZ, u).astype(BF)
            sends.append(d_copy(i))
            sends[-1].start()

    def x_copy(e, i):
        src = (x + (0, 0, 3, 1)[i]) % NX
        part = finx.at[e, src] if i < 2 else finx.at[e, src, pl.ds((i - 2) * 4, 4)]
        return copy(part, part, XA + e * 4 + i, xdev((1, 3, 1, 3)[i]))

    def to_owners(e, act):
        rows = pl.ds(pl.multiple_of(core * 64 + e * HALF, HALF), HALF)
        for dx in range(NX):
            for h in range(2):
                tx = (x + dx) % NX
                src, dst = finx.at[e, x, tx * 2 + h], kvg.at[x, rows]
                if dx > 0:
                    act(copy(src, dst, KVR + e, dev(tx, z, h, lo, hi)))
                else:
                    mine = own & (hi == h)

                    @pl.when(jnp.logical_not(mine))
                    def _():
                        act(copy(src, dst, KVR + e, dev(tx, z, h, lo, hi)))

                    @pl.when(mine)
                    def _():
                        act(pltpu.make_async_copy(src, dst, rsem.at[KVR + e]))

    def r_end(e):
        if e == 0:
            for i in range(1, NZ):
                d_copy(i).wait_recv()
        for u in range(2):
            part = slice(u * 4, u * 4 + 4)
            t = terms(e, z, u)
            if e == 0:
                for i in range(1, NZ):
                    t = t + d_rx[i - 1, part].astype(F32)
            else:
                for d in range(2):
                    r_copy(d, 3, u).wait_recv()
                    t = t + rs_rx[d, 3, u].astype(F32)
            finx[e, x, part] = t.astype(BF)
        for i in range(2):
            sends.append(x_copy(e, i))
            sends[-1].start()
        to_owners(e, start)

    def x_forward(e):
        for i in range(2):
            x_copy(e, i).wait_recv()
            sends.append(x_copy(e, 2 + i))
            sends[-1].start()

    def turn_hidden():
        arrived(hid_buf, HID)
        for e in range(2):
            for i in range(4):
                cols = slice(i * 128, (i + 1) * 128)
                part = hid_buf[:, e * HALF : (e + 1) * HALF, cols].reshape(8 * HALF, 128)
                hid_t[e, cols, :] = part.astype(F32).T.astype(BF)

    z_end(0)
    sort_kv(0)
    to_groups(2, start)
    diagonal(0)
    z_step(1, 2)
    at = below(0, 2, (0, 1))
    z_step(1, 3)
    below(0, 5, at)

    d_send()
    z_end(1)
    sort_kv(1)
    diagonal(1)
    below(1, 7, (0, 1))
    r_step(0)
    r_end(0)

    def place_q(blk, c):
        for j in range(4):
            t = (dqt[blk, :, j * 128 : (j + 1) * 128] * 0.125).T
            for o in range(2):
                dqs[blk * 8 + j * 2 + o] = jnp.concatenate(
                    [t[o * 64 + h * 16 : o * 64 + h * 16 + 16] for h in range(4)], axis=1
                )
        return c

    lax.fori_loop(0, 8, place_q, 0)
    r_step(1)

    def give_q(i, c):
        for j in range(4):
            k = i * 4 + j
            dqs_tx[k] = dqs[stored[0, k * 2 + core]]
        return c

    lax.fori_loop(0, 8, give_q, 0)
    sends.append(copy(dqs_tx, dqs_rx, DQS, sib))
    sends[-1].start()
    x_forward(0)
    r_step(2)
    turn_hidden()
    r_step(3)

    def c_copy(i):
        g = (x + i) % NX
        return copy(wpart.at[1 - core, g], c_rx.at[g], CX + i, sib)

    def grad_w(e, i):
        g = (x + i) % NX
        r = dot(hid_t[e], finx[e, g].reshape(8 * HALF, 128)).reshape(32, 2, 8, 128)
        for c in range(2):
            part = r[:, c].reshape(256, 128)
            wpart[c, g] = part if e == 0 else wpart[c, g] + part
        if e == 1:
            sends.append(c_copy(i))
            sends[-1].start()

    for i in range(2):
        x_copy(0, 2 + i).wait_recv()
    for i in range(4):
        grad_w(0, i)
    r_end(1)

    arrived(dqs_rx, DQS)

    def add_q(i, c):
        for j in range(4):
            k = i * 4 + j
            dq_tx[k] = (dqs[stored[0, k * 2 + 1 - core]] + dqs_rx[k]).astype(BF)
        return c

    lax.fori_loop(0, 8, add_q, 0)
    rows, cols = pl.ds(pl.multiple_of(z * 16, 16), 16), pl.ds(pl.multiple_of(x * 256, 256), 256)

    def q_return(i):
        tx, tz = (x + i // NZ) % NX, (z + i) % NZ
        return copy(dq_tx.at[tx * 8 + tz], dq_out.at[rows, cols], DQ, dev(tx, tz, 1 - core, lo, hi))

    def return_q(i, c):
        q_return(i).start()
        return c

    lax.fori_loop(0, 32, return_q, 0)

    grad_w(1, 0)
    x_forward(1)
    grad_w(1, 3)
    grad_w(1, 1)
    for i in range(2):
        x_copy(1, 2 + i).wait_recv()
    grad_w(1, 2)
    for i in range(4):
        c_copy(i).wait_recv()

    def w_sum(g):
        return (wpart[core, g] + c_rx[g]).reshape(32, 8, 128)

    for i in range(2):
        w_tx[:, :, i * 128 : (i + 1) * 128] = jnp.concatenate([w_sum(i), w_sum(2 + i)], axis=1).astype(BF)

    def w_copy(i):
        tx, tz = (x + i // NZ) % NX, (z + i) % NZ
        return copy(w_tx.at[tx * 8 + tz], w_rx.at[z * 4 + hi * 2 + lo], WR, w_to(i))

    def send_w(i, c):
        w_copy(i).start()
        return c

    @pl.when(jnp.logical_not(stays))
    def _():
        w_copy(0).start()

    @pl.when(stays)
    def _():
        pltpu.make_async_copy(w_tx.at[x * 8 + z], w_rx.at[z * 4 + hi * 2 + lo], rsem.at[WR]).start()

    lax.fori_loop(1, 32, send_w, 0)

    for e in range(2):
        arrived(kvg.at[pl.ds(0, 2)], KVR + e)

    kv_grad = jnp.concatenate([kvg[g, :, :64] for g in range(4)] + [kvg[g, :, 64:] for g in range(4)], axis=1)
    for i in range(4):
        in_out[:, i * 512 : (i + 1) * 512] = lax.dot_general(
            kv_grad, w_all[i], NT, preferred_element_type=F32
        ).astype(BF)

    for i, buf in enumerate(bufs):
        copy(buf.at[got], buf.at[got], Q + i, sib).wait_send()
    copy(dq_tx, dq_tx, DQ, sib).wait_send()
    arrived(dq_tx, DQ)
    for c in sends:
        c.wait_send()

    def sent(c):
        if c.is_remote:
            c.wait_send()

    for i in range(3):
        to_groups(i, sent)
    for e in range(2):
        to_owners(e, sent)

    arrived(w_rx, WR)

    def add_w(i, t):
        return t + w_rx[i].astype(F32)

    total = lax.fori_loop(0, 32, add_w, jnp.zeros((16, 256), F32))
    groups = [total[r : r + 8, c : c + 128] for r in (0, 8) for c in (0, 128)]
    wg_out[...] = jnp.concatenate([g[:, :64] for g in groups] + [g[:, 64:] for g in groups], axis=1)

    @pl.when(stays)
    def _():
        part = w_tx.at[pl.ds(0, 31)]
        copy(part, part, WR, sib).wait_send()

    @pl.when(jnp.logical_not(stays))
    def _():
        copy(w_tx, w_tx, WR, sib).wait_send()


def backward(hid, w, q, do, stat, order):
    v = pltpu.VMEM
    return pl.pallas_call(
        backward_kernel,
        name="backward",
        out_shape=(
            jax.ShapeDtypeStruct((128, 1024), BF),
            jax.ShapeDtypeStruct((128, 2048), BF),
            jax.ShapeDtypeStruct((8, 512), F32),
        ),
        in_specs=[VMEM] * 6,
        out_specs=[VMEM] * 3,
        scratch_shapes=[
            v((1, 64), jnp.int32),
            v((1, 64), jnp.int32),
            v((64, 128), jnp.int32),
            pltpu.SMEM((1, 64), jnp.int32),
            pltpu.SMEM((64, 128), jnp.int32),
            v((4, 512, 512), BF),
            v((128, 512), F32),
            v((4, 128, 128), BF),
            v((64, 16, 256), BF),
            v((64, 16, 256), BF),
            v((64, 1, 128), F32),
            v((64, HALF, 128), BF),
            v((64, HALF, 128), BF),
            v((8, 64, 512), BF),
            v((8, 512, 128), BF),
            v((8, 512, 128), BF),
            v((8, 8 * HALF, 128), BF),
            v((8, 64, 8 * HALF), BF),
            v((8, 1, 512), F32),
            v((8, 1, 512), F32),
            v((8, 64, 512), F32),
            v((2, 64, HALF, 128), F32),
            v((4, 8 * HALF, 512), BF),
            v((4, 8 * HALF, 512), BF),
            v((64, 16, 256), F32),
            v((32, 16, 256), F32),
            v((32, 16, 256), F32),
            v((32, 16, 256), BF),
            v((7, 8, HALF, 128), BF),
            v((7, 8, HALF, 128), BF),
            v((2, 4, 2, 4, HALF, 128), BF),
            v((2, 4, 2, 4, HALF, 128), BF),
            v((2, 4, 8, HALF, 128), BF),
            v((4, 128, 128), BF),
            v((2, 512, 8 * HALF), BF),
            v((2, 4, 256, 128), F32),
            v((4, 256, 128), F32),
            v((32, 16, 256), BF),
            v((32, 16, 256), BF),
            pltpu.SemaphoreType.DMA((N_SEMS + 1,)),
            pltpu.SemaphoreType.DMA((N_SEMS,)),
        ],
        compiler_params=pltpu.CompilerParams(
            collective_id=0, has_side_effects=True, vmem_limit_bytes=56 * 2**20
        ),
    )(hid, w, q, do, stat, order)


def shards(hidden, queries, attn_out, grad_out, log_sums, block_order, w_kv):
    delta = jnp.sum(
        (grad_out[0].astype(F32) * attn_out[0].astype(F32)).reshape(128, Q_HEADS, HEAD_DIM), axis=2
    ).T

    stat = jnp.stack([log_sums[0], delta]).reshape(2, 4, 4, 8, 16).transpose(1, 3, 0, 2, 4).reshape(4, 8, 1, 128)
    dq_out, in_out, wg = backward(hidden[0], w_kv, queries[0], grad_out[0], stat, block_order)
    return dq_out[None], in_out[None], wg


def solution(mesh):
    return jax.shard_map(
        shards,
        mesh=mesh,
        in_specs=(
            P("fsdp", "ctx", None),
            P("fsdp", "ctx", None),
            P("fsdp", "ctx", None),
            P("fsdp", "ctx", None),
            P("fsdp", None, "ctx"),
            P("fsdp", None),
            P("fsdp", None),
        ),
        out_specs=(P("fsdp", "ctx", None), P("fsdp", "ctx", None), P(("fsdp", "ctx"), None)),
        check_vma=False,
    )
```

```python
import functools

import jax
import jax.numpy as jnp
from jax import lax
from jax.experimental import pallas as pl
from jax.experimental.pallas import tpu as pltpu
from jax.sharding import PartitionSpec as P

BF, F32 = jnp.bfloat16, jnp.float32
NT = (((1,), (1,)), ((), ()))
TN = (((0,), (0,)), ((), ()))
MESH = pl.DeviceIdType.MESH
Q_HEADS, KV_HEADS, HEAD_DIM = 16, 4, 64
NX, NZ = 4, 8
VMEM = pl.BlockSpec(memory_space=pltpu.VMEM)


def place():
    f, c = lax.axis_index("fsdp"), lax.axis_index("ctx")
    return c // 16, (c // 2) % 8, c % 2, f // 2, f % 2


def dev(x, z, hi, lo, core):
    return {"fsdp": lo * 2 + core, "ctx": (x * 8 + z) * 2 + hi}


def rcopy(src, dst, send, recv, to):
    return pltpu.make_async_remote_copy(
        src_ref=src, dst_ref=dst, send_sem=send, recv_sem=recv, device_id=to, device_id_type=MESH
    )


def greet(to):
    pl.semaphore_signal(pltpu.get_barrier_semaphore(), inc=1, device_id=to, device_id_type=MESH)

META, W, WF, Q, QF, KV, HID, ZG, ZR, DQS, DQ, KVR, XA, CX, WR = (
    0, 98, 103, 6, 9, 12, 16, 17, 49, 81, 82, 83, 85, 93, 97
)
N_SEMS = 107
HALF = 32


def backward_kernel(
    hid, w, q, do, ao, ls, mine_order,
    dq_out, in_out, wg_out,
    stat, sib_order, stored_vm, sorted_vm, stored, sorted_, w_all, acc, kvs, q_buf, do_buf, stat_buf, kv_buf0, kv_buf1, hid_buf,
    qz, dz, ks, kts, lse, dlt, dqt, dkv, pbufs, dbufs,
    dqs, dqs_tx, dqs_rx, dq_tx, d_tx, d_rx, rs_tx, rs_rx, finx, kvg, hid_t, wpart, c_rx, w_tx, w_rx,
    ssem, rsem,
):
    x, z, hi, lo, core = place()
    f = lo * 2 + core
    sib = dev(x, z, hi, lo, 1 - core)
    near = dev(x, z, hi, 1 - lo, core)
    far = dev(x, z, 1 - hi, 1 - lo, core)
    own = hi == core

    def xdev(i):
        return dev((x + i) % NX, z, hi, lo, core)

    def zdev(i):
        return dev(x, (z + i) % NZ, hi, lo, core)

    def copy(src, dst, sem, to):
        return rcopy(src, dst, ssem.at[sem], rsem.at[sem], to)

    def arrived(ref, sem):
        rcopy(ref, ref, ssem.at[sem], rsem.at[sem], sib).wait_recv()

    for to in [sib, near, far, xdev(1), xdev(3)] + [zdev(i) for i in range(1, NZ)]:
        greet(to)

    def greet_q(i, c):
        greet(dev((x + i // NZ) % NX, (z + i) % NZ, 1 - core, lo, hi))
        return c

    lax.fori_loop(0, 32, greet_q, 0)

    def greet_kv(i, c):
        dx, h = i // 2, i % 2

        @pl.when(jnp.logical_not((dx == 0) & own & (h == hi)))
        def _():
            greet(dev((x + dx) % NX, z, h, lo, hi))

        return c

    lax.fori_loop(0, 8, greet_kv, 0)

    stays = own & (x // 2 == lo) & (x % 2 == core)

    def w_from(i):
        return dev(f, (z + i) % NZ, (hi + i // 16) % 2, (lo + i // 8) % 2, hi)

    def w_to(i):
        return dev((x + i // NZ) % NX, (z + i) % NZ, core, x // 2, x % 2)

    def greet_w(i, c):
        @pl.when(jnp.logical_not(stays & (i == 0)))
        def _():
            greet(w_from(i))

        return c

    lax.fori_loop(0, 32, greet_w, 0)
    pl.semaphore_wait(
        pltpu.get_barrier_semaphore(), 12 + 32 + 8 + 32 - own.astype(jnp.int32) - stays.astype(jnp.int32)
    )

    w_own = pltpu.make_async_copy(w, w_all.at[f], ssem.at[N_SEMS])
    w_own.start()
    quarter = w.shape[0] // 4

    def w_rows(i):
        return pl.ds(i * quarter, quarter)

    sends = [
        copy(w.at[w_rows(i)], w_all.at[f, w_rows(i)], W + i, far if i % 2 else near) for i in range(4)
    ]
    sends.append(copy(w, w_all.at[f], W + 4, sib))
    sends.append(copy(mine_order, sib_order, META, sib))
    for c in sends:
        c.start()

    slot = hi * 32 + x * 8 + z

    def q_copies(i):
        tx, tz = (x + i // NZ) % NX, (z + i) % NZ
        to = dev(tx, tz, core, lo, 1 - hi)
        rows, cols = pl.ds(pl.multiple_of(tz * 16, 16), 16), pl.ds(pl.multiple_of(tx * 256, 256), 256)
        return (
            copy(q.at[rows, cols], q_buf.at[slot], Q, to),
            copy(do.at[rows, cols], do_buf.at[slot], Q + 1, to),
        )

    def send_q(i, c):
        for one in q_copies(i):
            one.start()
        return c

    lax.fori_loop(0, 32, send_q, 0)

    prod = do[...].astype(F32) * ao[...].astype(F32)
    heads = lax.broadcasted_iota(jnp.int32, (Q_HEADS, Q_HEADS * HEAD_DIM), 0)
    pick = (lax.broadcasted_iota(jnp.int32, heads.shape, 1) // HEAD_DIM == heads).astype(F32).astype(BF)
    delta = jnp.zeros((Q_HEADS, 128), F32)
    for _ in range(3):
        term = prod.astype(BF)
        delta = delta + lax.dot_general(pick, term, NT, preferred_element_type=F32)
        prod = prod - term.astype(F32)
    turned = [[t] + [pltpu.roll(t, 16 * s, 1) for s in range(1, 8)] for t in (ls[...], delta)]
    head_of = lax.broadcasted_iota(jnp.int32, (Q_HEADS, 128), 0) % 4
    lanes_of = lax.broadcasted_iota(jnp.int32, (Q_HEADS, 128), 1) // 16
    for tz in range(NZ):
        row = jnp.zeros((Q_HEADS, 128), F32)
        for k in range(2):
            for h in range(4):
                row = jnp.where(
                    (head_of == h) & (lanes_of == h + 4 * k), turned[k][(h + 4 * k - tz) % 8], row
                )
        row = row + pltpu.roll(row, Q_HEADS - 1, 0)
        row = row + pltpu.roll(row, Q_HEADS - 2, 0)
        for g in range(4):
            stat[g, tz] = row[4 * g : 4 * g + 1, :]

    def send_stat(i, c):
        tx, tz = (x + i // NZ) % NX, (z + i) % NZ
        copy(stat.at[tx, tz], stat_buf.at[slot], Q + 2, dev(tx, tz, core, lo, 1 - hi)).start()
        return c

    lax.fori_loop(0, 32, send_stat, 0)

    def project(chunk):
        cols = pl.ds(pl.multiple_of(chunk * 512, 512), 512)
        return jnp.dot(hid[:, cols], w_all[chunk], preferred_element_type=F32)

    w_own.wait()
    acc[...] = project(f)
    arrived(w_all.at[0], W + 4)
    acc[...] += project(lo * 2 + 1 - core)
    other, last = (1 - lo) * 2 + core, (1 - lo) * 2 + 1 - core
    for i in range(4):
        part = w_all.at[other, w_rows(i)]
        arrived(part, W + i)
        sends.append(copy(part, part, WF + i, sib))
        sends[-1].start()
    acc[...] += project(other)
    for i in range(4):
        arrived(w_all.at[last, w_rows(i)], WF + i)
    key_vals = (acc[...] + project(last)).astype(BF)
    for g in range(KV_HEADS):
        kvs[g] = jnp.concatenate(
            [key_vals[:, g * 64 : g * 64 + 64], key_vals[:, 256 + g * 64 : 320 + g * 64]], axis=1
        )

    kv_buf = (kv_buf0, kv_buf1)

    def to_group(dx, j, which):
        tx = (x + dx) % NX
        to = dev(tx, z, core, lo, j)
        mine = x * 2 + hi
        if which < 2:
            rows = pl.ds(j * 64 + which * HALF, HALF)
            return (kvs.at[tx, rows], kv_buf[which].at[z * 8 + mine], KV + which * 2 + x // 2), to
        rows, cols = pl.ds(j * 64, 64), pl.ds(pl.multiple_of(tx * 512, 512), 512)
        return (hid.at[rows, cols], hid_buf.at[mine], HID), to

    def to_groups(which, act):
        for dx in range(NX):
            for j in range(2):
                piece, to = to_group(dx, j, which)
                if dx > 0:
                    act(copy(*piece, to))
                else:
                    mine = own & (core == j)

                    @pl.when(jnp.logical_not(mine))
                    def _():
                        act(copy(*piece, to))

                    @pl.when(mine)
                    def _():
                        src, dst, sem = piece
                        act(pltpu.make_async_copy(src, dst, rsem.at[sem]))

    def start(c):
        c.start()

    to_groups(0, start)
    to_groups(1, start)

    def z_part(src_z, u):
        return pl.ds(pl.multiple_of(src_z * 8 + u * 4, 4), 4)

    def z_copy(e, d, s, u):
        part = kv_buf[e].at[z_part((z + 8 - s) % NZ if d == 0 else (z + s) % NZ, u)]
        return copy(part, part, ZG + e * 16 + (d * 4 + s) * 2 + u, zdev(1) if d == 0 else zdev(7))

    def z_step(e, s):
        for u in range(2):
            if s == 0:
                arrived(kv_buf[e].at[pl.ds(0, 4)], KV + e * 2 + u)
            for d in range(2):
                if s == 3 and u != d:
                    continue
                if s:
                    z_copy(e, d, s - 1, u).wait_recv()
                sends.append(z_copy(e, d, s, u))
                sends[-1].start()

    def z_end(e):
        for d, s, u in ((0, 2, 1), (1, 2, 0), (0, 3, 0), (1, 3, 1)):
            z_copy(e, d, s, u).wait_recv()

    z_step(0, 0)
    z_step(0, 1)
    z_step(1, 0)
    z_step(0, 2)
    z_step(0, 3)

    got = pl.ds(pl.multiple_of((1 - core) * 32, 32), 32)
    theirs = pl.ds(pl.multiple_of(core * 32, 32), 32)
    bufs = (q_buf, do_buf, stat_buf)
    for i, buf in enumerate(bufs):
        arrived(buf.at[got], Q + i)
        sends.append(copy(buf.at[got], buf.at[got], QF + i, sib))
        sends[-1].start()

    arrived(sib_order, META)
    there = jnp.where(own, mine_order[...], sib_order[...])
    ids = lax.broadcasted_iota(jnp.int32, (64, 64), 1)
    back = jnp.max(jnp.where(there == lax.broadcasted_iota(jnp.int32, (64, 64), 0), ids, 0), axis=1, keepdims=True)
    stored_vm[...] = there
    sorted_vm[...] = jnp.broadcast_to(back, (64, 128))
    for vm, sm in ((stored_vm, stored), (sorted_vm, sorted_)):
        c = pltpu.make_async_copy(vm, sm, ssem.at[N_SEMS])
        c.start()
        c.wait()

    for i, buf in enumerate(bufs):
        arrived(buf.at[theirs], QF + i)

    low = lax.broadcasted_iota(jnp.int32, (16, 128), 1) < 64
    low1 = lax.broadcasted_iota(jnp.int32, (1, 128), 1) < 64

    def sort_q(blk, c):
        stats = []
        for off in range(8):
            b = sorted_[blk * 8 + off, 0]
            s = (b % 2) * 32 + b // 2
            for hp in range(2):
                qq = q_buf[s, :, hp * 128 : (hp + 1) * 128].astype(F32) * 0.125
                dd = do_buf[s, :, hp * 128 : (hp + 1) * 128].astype(F32)
                for ho in range(2):
                    rows = slice(off * 64 + hp * 32 + ho * 16, off * 64 + hp * 32 + ho * 16 + 16)
                    qh = qq if ho == 0 else pltpu.roll(qq, 64, 1)
                    dh = dd if ho == 1 else pltpu.roll(dd, 64, 1)
                    qz[blk, rows, :] = jnp.where(low, qh, 0.0).astype(BF)
                    dz[blk, rows, :] = jnp.where(low, 0.0, dh).astype(BF)
            stats.append(stat_buf[s])
        for j in range(4):
            a, b = stats[2 * j], stats[2 * j + 1]
            lse[blk, :, j * 128 : (j + 1) * 128] = jnp.where(low1, a, pltpu.roll(b, 64, 1))
            dlt[blk, :, j * 128 : (j + 1) * 128] = jnp.where(low1, pltpu.roll(a, 64, 1), b)
        dqt[blk] = jnp.zeros((64, 512), F32)
        return c

    lax.fori_loop(0, 8, sort_q, 0)
    z_step(1, 1)

    def sort_kv(e):
        def one(blk, c):
            for off in range(8):
                b = sorted_[blk * 8 + off, 0]
                ks[blk, off * HALF : (off + 1) * HALF, :] = kv_buf[e][((b // 2) % 8) * 8 + (b // 16) * 2 + b % 2]
            kts[blk] = ks[blk].astype(F32).T[:64].astype(BF)
            return c

        lax.fori_loop(0, 8, one, 0)

    def probs(m, c, t, e=None):
        for n, qs in ((256, slice(0, 512)),) if e is None else ((128, slice(0, 256)), (256, slice(256, 512))):
            keys = slice(0, n)
            kv = ks[m, keys, :]
            p = jnp.exp(lax.dot_general(kv, qz[c, qs], NT, preferred_element_type=F32) - lse[c, :, qs])
            if e is not None:
                kp = lax.broadcasted_iota(jnp.int32, p.shape, 0)
                qp = lax.broadcasted_iota(jnp.int32, p.shape, 1) + qs.start
                kpos = (kp // HALF) * 128 + (kp % HALF) + core * 64 + e * HALF
                qpos = (qp // 64) * 128 + (qp % 16) + z * 16
                p = jnp.where(kpos <= qpos, p, 0.0)
            dp = lax.dot_general(kv, dz[c, qs], NT, preferred_element_type=F32)
            dbufs[t, keys, qs] = (p * (dp - dlt[c, :, qs])).astype(BF)
            pbufs[t, keys, qs] = p.astype(BF)

    def dot(a, b):
        return jnp.dot(a, b, preferred_element_type=F32)

    def diag_grads(e, m, t):
        top = dot(dbufs[t, :128, :], qz[m]) + dot(pbufs[t, :128, :], dz[m])
        bottom = dot(dbufs[t, 128:, 256:], qz[m, 256:]) + dot(pbufs[t, 128:, 256:], dz[m, 256:])
        dkv[e, pl.ds(m * 8, 4)] = top.reshape(4, HALF, 128)
        dkv[e, pl.ds(m * 8 + 4, 4)] = bottom.reshape(4, HALF, 128)
        dqt[m, :, :256] += dot(kts[m, :, :128], dbufs[t, :128, :256])
        dqt[m, :, 256:] += dot(kts[m], dbufs[t, :, 256:])

    def grads(e, m, c, t):
        ds, p = dbufs[t], pbufs[t]
        dkv[e, pl.ds(m * 8, 8)] += (dot(ds, qz[c]) + dot(p, dz[c])).reshape(8, HALF, 128)
        dqt[c] += dot(kts[m], ds)

    def diagonal(e):
        def one(i, c):
            for t in range(4):
                probs(4 * i + t, 4 * i + t, t, e)
            for t in range(4):
                diag_grads(e, 4 * i + t, t)
            return c

        lax.fori_loop(0, 2, one, 0)

    def following(m, c):
        wrap = c == 7
        return jnp.where(wrap, m + 1, m), jnp.where(wrap, jnp.minimum(m + 2, 7), c + 1)

    def below(e, n, at, beside=None):
        def four(i, at):
            if beside is not None:
                beside(i)
            tiles = [at]
            for t in range(4):
                probs(*tiles[t], t)
                tiles.append(following(*tiles[t]))
            for t in range(4):
                grads(e, *tiles[t], t)
            return tiles[4]

        return lax.fori_loop(0, n, four, at)

    def r_copy(d, s, u):
        return copy(
            rs_tx.at[d, s, u], rs_rx.at[d, s, u], ZR + 16 + (d * 4 + s) * 2 + u, zdev(1) if d == 0 else zdev(7)
        )

    def terms(e, tz, u):
        parts = []
        for i in range(4):
            b = ((u * 2 + i // 2) * 8 + tz) * 2 + i % 2
            parts.append(dkv[e, stored[0, b]][None])
        return jnp.concatenate(parts, axis=0)

    def r_step(s):
        for u in range(2):
            for d in range(2):
                if s == 0 and u != d:
                    continue
                t = terms(1, (z + 4 - s) % NZ if d == 0 else (z + 4 + s) % NZ, u)
                if s > 1 or (s == 1 and u == d):
                    r_copy(d, s - 1, u).wait_recv()
                    t = t + rs_rx[d, s - 1, u].astype(F32)
                rs_tx[d, s, u] = t.astype(BF)
                sends.append(r_copy(d, s, u))
                sends[-1].start()

    def d_copy(i):
        return copy(d_tx.at[i - 1], d_rx.at[i - 1], ZR + i, zdev(i))

    def d_send():
        for i in (4, 3, 5, 2, 6, 1, 7):
            for u in range(2):
                d_tx[i - 1, u * 4 : u * 4 + 4] = terms(0, (z + i) % NZ, u).astype(BF)
            sends.append(d_copy(i))
            sends[-1].start()

    def x_copy(e, i):
        src = (x + (0, 0, 3, 1)[i]) % NX
        part = finx.at[e, src] if i < 2 else finx.at[e, src, pl.ds((i - 2) * 4, 4)]
        return copy(part, part, XA + e * 4 + i, xdev((1, 3, 1, 3)[i]))

    def to_owners(e, act):
        rows = pl.ds(pl.multiple_of(core * 64 + e * HALF, HALF), HALF)
        for dx in range(NX):
            for h in range(2):
                tx = (x + dx) % NX
                src, dst = finx.at[e, x, tx * 2 + h], kvg.at[x, rows]
                if dx > 0:
                    act(copy(src, dst, KVR + e, dev(tx, z, h, lo, hi)))
                else:
                    mine = own & (hi == h)

                    @pl.when(jnp.logical_not(mine))
                    def _():
                        act(copy(src, dst, KVR + e, dev(tx, z, h, lo, hi)))

                    @pl.when(mine)
                    def _():
                        act(pltpu.make_async_copy(src, dst, rsem.at[KVR + e]))

    def r_end(e):
        if e == 0:
            for i in range(1, NZ):
                d_copy(i).wait_recv()
        for u in range(2):
            part = slice(u * 4, u * 4 + 4)
            t = terms(e, z, u)
            if e == 0:
                for i in range(1, NZ):
                    t = t + d_rx[i - 1, part].astype(F32)
            else:
                for d in range(2):
                    r_copy(d, 3, u).wait_recv()
                    t = t + rs_rx[d, 3, u].astype(F32)
            finx[e, x, part] = t.astype(BF)
        for i in range(2):
            sends.append(x_copy(e, i))
            sends[-1].start()
        to_owners(e, start)

    def x_forward(e):
        for i in range(2):
            x_copy(e, i).wait_recv()
            sends.append(x_copy(e, 2 + i))
            sends[-1].start()

    def turn_hidden(i):
        e, c = i // 4, i % 4
        cols = pl.ds(pl.multiple_of(c * 128, 128), 128)
        part = hid_buf[:, pl.ds(pl.multiple_of(e * HALF, HALF), HALF), cols].reshape(8 * HALF, 128)
        hid_t[e, cols, :] = part.astype(F32).T.astype(BF)

    def place_q(blk):
        for j in range(4):
            t = (dqt[blk, :, j * 128 : (j + 1) * 128] * 0.125).T
            for o in range(2):
                dqs[blk * 8 + j * 2 + o] = jnp.concatenate(
                    [t[o * 64 + h * 16 : o * 64 + h * 16 + 16] for h in range(4)], axis=1
                )

    z_end(0)
    sort_kv(0)
    to_groups(2, start)
    diagonal(0)
    z_step(1, 2)
    at = below(0, 2, (0, 1))
    z_step(1, 3)
    below(0, 5, at)

    d_send()
    z_end(1)
    sort_kv(1)
    diagonal(1)
    arrived(hid_buf, HID)
    turn_hidden(7)

    def beside(i):
        turn_hidden(i)
        place_q(jnp.maximum(i - 1, 0))

    below(1, 7, (0, 1), beside)
    r_step(0)
    r_end(0)

    for blk in (6, 7):
        place_q(blk)
    r_step(1)

    def give_q(i, c):
        for j in range(4):
            k = i * 4 + j
            dqs_tx[k] = dqs[stored[0, k * 2 + core]]
        return c

    lax.fori_loop(0, 8, give_q, 0)
    sends.append(copy(dqs_tx, dqs_rx, DQS, sib))
    sends[-1].start()
    x_forward(0)
    r_step(2)
    arrived(dqs_rx, DQS)

    def add_q(i, c):
        for j in range(4):
            k = i * 4 + j
            dq_tx[k] = (dqs[stored[0, k * 2 + 1 - core]] + dqs_rx[k]).astype(BF)
        return c

    lax.fori_loop(0, 8, add_q, 0)
    rows, cols = pl.ds(pl.multiple_of(z * 16, 16), 16), pl.ds(pl.multiple_of(x * 256, 256), 256)

    def q_return(i):
        tx, tz = (x + i // NZ) % NX, (z + i) % NZ
        return copy(dq_tx.at[tx * 8 + tz], dq_out.at[rows, cols], DQ, dev(tx, tz, 1 - core, lo, hi))

    def return_q(i, c):
        q_return(i).start()
        return c

    lax.fori_loop(0, 32, return_q, 0)

    r_step(3)

    def c_copy(i):
        g = (x + i) % NX
        return copy(wpart.at[1 - core, g], c_rx.at[g], CX + i, sib)

    def grad_w(e, i):
        g = (x + i) % NX
        r = dot(hid_t[e], finx[e, g].reshape(8 * HALF, 128)).reshape(32, 2, 8, 128)
        for c in range(2):
            part = r[:, c].reshape(256, 128)
            wpart[c, g] = part if e == 0 else wpart[c, g] + part
        if e == 1:
            sends.append(c_copy(i))
            sends[-1].start()

    for i in range(2):
        x_copy(0, 2 + i).wait_recv()
    for i in range(4):
        grad_w(0, i)
    r_end(1)

    grad_w(1, 0)
    x_forward(1)
    grad_w(1, 3)
    grad_w(1, 1)
    for i in range(2):
        x_copy(1, 2 + i).wait_recv()
    grad_w(1, 2)
    for i in range(4):
        c_copy(i).wait_recv()

    def w_sum(g):
        return (wpart[core, g] + c_rx[g]).reshape(32, 8, 128)

    for i in range(2):
        w_tx[:, :, i * 128 : (i + 1) * 128] = jnp.concatenate([w_sum(i), w_sum(2 + i)], axis=1).astype(BF)

    def w_copy(i):
        tx, tz = (x + i // NZ) % NX, (z + i) % NZ
        return copy(w_tx.at[tx * 8 + tz], w_rx.at[z * 4 + hi * 2 + lo], WR, w_to(i))

    def send_w(i, c):
        w_copy(i).start()
        return c

    @pl.when(jnp.logical_not(stays))
    def _():
        w_copy(0).start()

    @pl.when(stays)
    def _():
        pltpu.make_async_copy(w_tx.at[x * 8 + z], w_rx.at[z * 4 + hi * 2 + lo], rsem.at[WR]).start()

    lax.fori_loop(1, 32, send_w, 0)

    for e in range(2):
        arrived(kvg.at[pl.ds(0, 2)], KVR + e)

    kv_grad = jnp.concatenate([kvg[g, :, :64] for g in range(4)] + [kvg[g, :, 64:] for g in range(4)], axis=1)
    for i in range(4):
        in_out[:, i * 512 : (i + 1) * 512] = lax.dot_general(
            kv_grad, w_all[i], NT, preferred_element_type=F32
        ).astype(BF)

    for i, buf in enumerate(bufs):
        copy(buf.at[got], buf.at[got], Q + i, sib).wait_send()
    copy(dq_tx, dq_tx, DQ, sib).wait_send()
    arrived(dq_tx, DQ)
    for c in sends:
        c.wait_send()

    def sent(c):
        if c.is_remote:
            c.wait_send()

    for i in range(3):
        to_groups(i, sent)
    for e in range(2):
        to_owners(e, sent)

    arrived(w_rx, WR)

    def add_w(i, t):
        return t + w_rx[i].astype(F32)

    total = lax.fori_loop(0, 32, add_w, jnp.zeros((16, 256), F32))
    groups = [total[r : r + 8, c : c + 128] for r in (0, 8) for c in (0, 128)]
    wg_out[...] = jnp.concatenate([g[:, :64] for g in groups] + [g[:, 64:] for g in groups], axis=1)

    @pl.when(stays)
    def _():
        part = w_tx.at[pl.ds(0, 31)]
        copy(part, part, WR, sib).wait_send()

    @pl.when(jnp.logical_not(stays))
    def _():
        copy(w_tx, w_tx, WR, sib).wait_send()


def backward(hid, w, q, do, ao, ls, order):
    v = pltpu.VMEM
    return pl.pallas_call(
        backward_kernel,
        name="backward",
        out_shape=(
            jax.ShapeDtypeStruct((128, 1024), BF),
            jax.ShapeDtypeStruct((128, 2048), BF),
            jax.ShapeDtypeStruct((8, 512), F32),
        ),
        in_specs=[VMEM] * 7,
        out_specs=[VMEM] * 3,
        scratch_shapes=[
            v((4, 8, 1, 128), F32),
            v((1, 64), jnp.int32),
            v((1, 64), jnp.int32),
            v((64, 128), jnp.int32),
            pltpu.SMEM((1, 64), jnp.int32),
            pltpu.SMEM((64, 128), jnp.int32),
            v((4, 512, 512), BF),
            v((128, 512), F32),
            v((4, 128, 128), BF),
            v((64, 16, 256), BF),
            v((64, 16, 256), BF),
            v((64, 1, 128), F32),
            v((64, HALF, 128), BF),
            v((64, HALF, 128), BF),
            v((8, 64, 512), BF),
            v((8, 512, 128), BF),
            v((8, 512, 128), BF),
            v((8, 8 * HALF, 128), BF),
            v((8, 64, 8 * HALF), BF),
            v((8, 1, 512), F32),
            v((8, 1, 512), F32),
            v((8, 64, 512), F32),
            v((2, 64, HALF, 128), F32),
            v((4, 8 * HALF, 512), BF),
            v((4, 8 * HALF, 512), BF),
            v((64, 16, 256), F32),
            v((32, 16, 256), F32),
            v((32, 16, 256), F32),
            v((32, 16, 256), BF),
            v((7, 8, HALF, 128), BF),
            v((7, 8, HALF, 128), BF),
            v((2, 4, 2, 4, HALF, 128), BF),
            v((2, 4, 2, 4, HALF, 128), BF),
            v((2, 4, 8, HALF, 128), BF),
            v((4, 128, 128), BF),
            v((2, 512, 8 * HALF), BF),
            v((2, 4, 256, 128), F32),
            v((4, 256, 128), F32),
            v((32, 16, 256), BF),
            v((32, 16, 256), BF),
            pltpu.SemaphoreType.DMA((N_SEMS + 1,)),
            pltpu.SemaphoreType.DMA((N_SEMS,)),
        ],
        compiler_params=pltpu.CompilerParams(
            collective_id=0, has_side_effects=True, vmem_limit_bytes=56 * 2**20
        ),
    )(hid, w, q, do, ao, ls, order)


def shards(hidden, queries, attn_out, grad_out, log_sums, block_order, w_kv):
    dq_out, in_out, wg = backward(hidden[0], w_kv, queries[0], grad_out[0], attn_out[0], log_sums[0], block_order)
    return dq_out[None], in_out[None], wg


def solution(mesh):
    return jax.shard_map(
        shards,
        mesh=mesh,
        in_specs=(
            P("fsdp", "ctx", None),
            P("fsdp", "ctx", None),
            P("fsdp", "ctx", None),
            P("fsdp", "ctx", None),
            P("fsdp", None, "ctx"),
            P("fsdp", None),
            P("fsdp", None),
        ),
        out_specs=(P("fsdp", "ctx", None), P("fsdp", "ctx", None), P(("fsdp", "ctx"), None)),
        check_vma=False,
    )
```

```python
import functools

import jax
import jax.numpy as jnp
from jax import lax
from jax.experimental import pallas as pl
from jax.experimental.pallas import tpu as pltpu
from jax.sharding import PartitionSpec as P

BF, F32 = jnp.bfloat16, jnp.float32
NT = (((1,), (1,)), ((), ()))
TN = (((0,), (0,)), ((), ()))
MESH = pl.DeviceIdType.MESH
Q_HEADS, KV_HEADS, HEAD_DIM = 16, 4, 64
NX, NZ = 4, 8
Z_STEPS = (4, 1, 7, 3, 5, 2, 6, 0)
VMEM = pl.BlockSpec(memory_space=pltpu.VMEM)


def place():
    f, c = lax.axis_index("fsdp"), lax.axis_index("ctx")
    return c // 16, (c // 2) % 8, c % 2, f // 2, f % 2


def dev(x, z, hi, lo, core):
    return {"fsdp": lo * 2 + core, "ctx": (x * 8 + z) * 2 + hi}


def rcopy(src, dst, send, recv, to):
    return pltpu.make_async_remote_copy(
        src_ref=src, dst_ref=dst, send_sem=send, recv_sem=recv, device_id=to, device_id_type=MESH
    )


def greet(to):
    pl.semaphore_signal(pltpu.get_barrier_semaphore(), inc=1, device_id=to, device_id_type=MESH)

META, W, WF, Q, QF, KV, HID, ZG, ZR, DQS, DQ, KVR, XA, CX, WR = (
    0, 98, 103, 6, 9, 12, 16, 17, 49, 81, 82, 83, 85, 93, 97
)
N_SEMS = 107
HALF = 32


def backward_kernel(
    hid, w, q, do, ao, ls, mine_order,
    dq_out, in_out, wg_out,
    stat, sib_order, stored_vm, sorted_vm, stored, sorted_, w_all, acc, kvs, q_buf, do_buf, stat_buf, kv_buf0, kv_buf1, hid_buf,
    qz, dz, ks, kts, lse, dlt, dqt, dkv, pbufs, dbufs,
    dqs, dqs_tx, dqs_rx, dq_tx, d_tx, d_rx, rs_tx, rs_rx, finx, kvg, hid_t, wpart, c_rx, w_tx, w_rx,
    ssem, rsem,
):
    x, z, hi, lo, core = place()
    f = lo * 2 + core
    sib = dev(x, z, hi, lo, 1 - core)
    near = dev(x, z, hi, 1 - lo, core)
    far = dev(x, z, 1 - hi, 1 - lo, core)
    own = hi == core

    def xdev(i):
        return dev((x + i) % NX, z, hi, lo, core)

    def zdev(i):
        return dev(x, (z + i) % NZ, hi, lo, core)

    def copy(src, dst, sem, to):
        return rcopy(src, dst, ssem.at[sem], rsem.at[sem], to)

    def arrived(ref, sem):
        rcopy(ref, ref, ssem.at[sem], rsem.at[sem], sib).wait_recv()

    for to in [sib, near, far, xdev(1), xdev(3)] + [zdev(i) for i in range(1, NZ)]:
        greet(to)

    def greet_q(i, c):
        for j in range(4):
            greet(dev((x + i // 2) % NX, (z + i * 4 + j) % NZ, 1 - core, lo, hi))
        return c

    lax.fori_loop(0, 8, greet_q, 0)

    def greet_kv(i, c):
        dx, h = i // 2, i % 2

        @pl.when(jnp.logical_not((dx == 0) & own & (h == hi)))
        def _():
            greet(dev((x + dx) % NX, z, h, lo, hi))

        return c

    lax.fori_loop(0, 8, greet_kv, 0)

    stays = own & (x // 2 == lo) & (x % 2 == core)

    def w_from(i):
        return dev(f, (z + i) % NZ, (hi + i // 16) % 2, (lo + i // 8) % 2, hi)

    def w_to(i):
        return dev((x + i // NZ) % NX, (z + i) % NZ, core, x // 2, x % 2)

    def greet_w(i, c):
        for j in range(4):
            greet(w_from(i * 4 + j))
        return c

    @pl.when(jnp.logical_not(stays))
    def _():
        greet(w_from(0))

    for i in range(1, 4):
        greet(w_from(i))
    lax.fori_loop(1, 8, greet_w, 0)
    pl.semaphore_wait(
        pltpu.get_barrier_semaphore(), 12 + 32 + 8 + 32 - own.astype(jnp.int32) - stays.astype(jnp.int32)
    )

    w_own = pltpu.make_async_copy(w, w_all.at[f], ssem.at[N_SEMS])
    w_own.start()
    quarter = w.shape[0] // 4

    def w_rows(i):
        return pl.ds(i * quarter, quarter)

    sends = [
        copy(w.at[w_rows(i)], w_all.at[f, w_rows(i)], W + i, far if i % 2 else near) for i in range(4)
    ]
    sends.append(copy(w, w_all.at[f], W + 4, sib))
    sends.append(copy(mine_order, sib_order, META, sib))
    for c in sends:
        c.start()

    slot = hi * 32 + x * 8 + z

    def q_copies(i):
        tx, tz = (x + i // NZ) % NX, (z + i) % NZ
        to = dev(tx, tz, core, lo, 1 - hi)
        rows, cols = pl.ds(pl.multiple_of(tz * 16, 16), 16), pl.ds(pl.multiple_of(tx * 256, 256), 256)
        return (
            copy(q.at[rows, cols], q_buf.at[slot], Q, to),
            copy(do.at[rows, cols], do_buf.at[slot], Q + 1, to),
        )

    def send_q(i, c):
        for j in Z_STEPS:
            for one in q_copies(i * NZ + j):
                one.start()
        return c

    lax.fori_loop(0, NX, send_q, 0)

    def project(chunk):
        cols = pl.ds(pl.multiple_of(chunk * 512, 512), 512)
        return jnp.dot(hid[:, cols], w_all[chunk], preferred_element_type=F32)

    w_own.wait()
    acc[...] = project(f)
    arrived(w_all.at[0], W + 4)
    acc[...] += project(lo * 2 + 1 - core)
    other, last = (1 - lo) * 2 + core, (1 - lo) * 2 + 1 - core
    for i in range(4):
        part = w_all.at[other, w_rows(i)]
        arrived(part, W + i)
        sends.append(copy(part, part, WF + i, sib))
        sends[-1].start()
    acc[...] += project(other)
    for i in range(4):
        arrived(w_all.at[last, w_rows(i)], WF + i)
    key_vals = (acc[...] + project(last)).astype(BF)
    for g in range(KV_HEADS):
        kvs[g] = jnp.concatenate(
            [key_vals[:, g * 64 : g * 64 + 64], key_vals[:, 256 + g * 64 : 320 + g * 64]], axis=1
        )

    kv_buf = (kv_buf0, kv_buf1)

    def to_group(dx, j, which):
        tx = (x + dx) % NX
        to = dev(tx, z, core, lo, j)
        mine = x * 2 + hi
        if which < 2:
            rows = pl.ds(j * 64 + which * HALF, HALF)
            return (kvs.at[tx, rows], kv_buf[which].at[z * 8 + mine], KV + which * 2 + x // 2), to
        rows, cols = pl.ds(j * 64, 64), pl.ds(pl.multiple_of(tx * 512, 512), 512)
        return (hid.at[rows, cols], hid_buf.at[mine], HID), to

    def to_groups(which, act):
        for dx in range(NX):
            for j in range(2):
                piece, to = to_group(dx, j, which)
                if dx > 0:
                    act(copy(*piece, to))
                else:
                    mine = own & (core == j)

                    @pl.when(jnp.logical_not(mine))
                    def _():
                        act(copy(*piece, to))

                    @pl.when(mine)
                    def _():
                        src, dst, sem = piece
                        act(pltpu.make_async_copy(src, dst, rsem.at[sem]))

    def start(c):
        c.start()

    to_groups(0, start)
    to_groups(1, start)

    prod = do[...].astype(F32) * ao[...].astype(F32)
    heads = lax.broadcasted_iota(jnp.int32, (Q_HEADS, Q_HEADS * HEAD_DIM), 0)
    pick = (lax.broadcasted_iota(jnp.int32, heads.shape, 1) // HEAD_DIM == heads).astype(F32).astype(BF)
    delta = jnp.zeros((Q_HEADS, 128), F32)
    for _ in range(3):
        term = prod.astype(BF)
        delta = delta + lax.dot_general(pick, term, NT, preferred_element_type=F32)
        prod = prod - term.astype(F32)
    turned = [[t] + [pltpu.roll(t, 16 * s, 1) for s in range(1, 8)] for t in (ls[...], delta)]
    head_of = lax.broadcasted_iota(jnp.int32, (Q_HEADS, 128), 0) % 4
    lanes_of = lax.broadcasted_iota(jnp.int32, (Q_HEADS, 128), 1) // 16
    for tz in range(NZ):
        row = jnp.zeros((Q_HEADS, 128), F32)
        for k in range(2):
            for h in range(4):
                row = jnp.where(
                    (head_of == h) & (lanes_of == h + 4 * k), turned[k][(h + 4 * k - tz) % 8], row
                )
        row = row + pltpu.roll(row, Q_HEADS - 1, 0)
        row = row + pltpu.roll(row, Q_HEADS - 2, 0)
        for g in range(4):
            stat[g, tz] = row[4 * g : 4 * g + 1, :]

    def send_stat(i, c):
        for j in Z_STEPS:
            tx, tz = (x + i) % NX, (z + j) % NZ
            copy(stat.at[tx, tz], stat_buf.at[slot], Q + 2, dev(tx, tz, core, lo, 1 - hi)).start()
        return c

    lax.fori_loop(0, NX, send_stat, 0)


    def z_part(src_z, u):
        return pl.ds(pl.multiple_of(src_z * 8 + u * 4, 4), 4)

    def z_copy(e, d, s, u):
        part = kv_buf[e].at[z_part((z + 8 - s) % NZ if d == 0 else (z + s) % NZ, u)]
        return copy(part, part, ZG + e * 16 + (d * 4 + s) * 2 + u, zdev(1) if d == 0 else zdev(7))

    def z_step(e, s):
        for u in range(2):
            if s == 0:
                arrived(kv_buf[e].at[pl.ds(0, 4)], KV + e * 2 + u)
            for d in range(2):
                if s == 3 and u != d:
                    continue
                if s:
                    z_copy(e, d, s - 1, u).wait_recv()
                sends.append(z_copy(e, d, s, u))
                sends[-1].start()

    def z_end(e):
        for d, s, u in ((0, 2, 1), (1, 2, 0), (0, 3, 0), (1, 3, 1)):
            z_copy(e, d, s, u).wait_recv()

    z_step(0, 0)
    z_step(0, 1)
    z_step(1, 0)
    z_step(0, 2)
    z_step(0, 3)

    got = pl.ds(pl.multiple_of((1 - core) * 32, 32), 32)
    theirs = pl.ds(pl.multiple_of(core * 32, 32), 32)
    bufs = (q_buf, do_buf, stat_buf)
    for i, buf in enumerate(bufs):
        arrived(buf.at[got], Q + i)
        sends.append(copy(buf.at[got], buf.at[got], QF + i, sib))
        sends[-1].start()

    arrived(sib_order, META)
    there = jnp.where(own, mine_order[...], sib_order[...])
    ids = lax.broadcasted_iota(jnp.int32, (64, 64), 1)
    back = jnp.max(jnp.where(there == lax.broadcasted_iota(jnp.int32, (64, 64), 0), ids, 0), axis=1, keepdims=True)
    stored_vm[...] = there
    sorted_vm[...] = jnp.broadcast_to(back, (64, 128))
    for vm, sm in ((stored_vm, stored), (sorted_vm, sorted_)):
        c = pltpu.make_async_copy(vm, sm, ssem.at[N_SEMS])
        c.start()
        c.wait()

    for i, buf in enumerate(bufs):
        arrived(buf.at[theirs], QF + i)

    low = lax.broadcasted_iota(jnp.int32, (16, 128), 1) < 64
    low1 = lax.broadcasted_iota(jnp.int32, (1, 128), 1) < 64

    def sort_q(blk, c):
        stats = []
        for off in range(8):
            b = sorted_[blk * 8 + off, 0]
            s = (b % 2) * 32 + b // 2
            for hp in range(2):
                qq = q_buf[s, :, hp * 128 : (hp + 1) * 128].astype(F32) * 0.125
                dd = do_buf[s, :, hp * 128 : (hp + 1) * 128].astype(F32)
                for ho in range(2):
                    rows = slice(off * 64 + hp * 32 + ho * 16, off * 64 + hp * 32 + ho * 16 + 16)
                    qh = qq if ho == 0 else pltpu.roll(qq, 64, 1)
                    dh = dd if ho == 1 else pltpu.roll(dd, 64, 1)
                    qz[blk, rows, :] = jnp.where(low, qh, 0.0).astype(BF)
                    dz[blk, rows, :] = jnp.where(low, 0.0, dh).astype(BF)
            stats.append(stat_buf[s])
        for j in range(4):
            a, b = stats[2 * j], stats[2 * j + 1]
            lse[blk, :, j * 128 : (j + 1) * 128] = jnp.where(low1, a, pltpu.roll(b, 64, 1))
            dlt[blk, :, j * 128 : (j + 1) * 128] = jnp.where(low1, pltpu.roll(a, 64, 1), b)
        dqt[blk] = jnp.zeros((64, 512), F32)
        return c

    lax.fori_loop(0, 8, sort_q, 0)
    z_step(1, 1)

    def sort_kv(e):
        def one(blk, c):
            for off in range(8):
                b = sorted_[blk * 8 + off, 0]
                ks[blk, off * HALF : (off + 1) * HALF, :] = kv_buf[e][((b // 2) % 8) * 8 + (b // 16) * 2 + b % 2]
            kts[blk] = ks[blk].astype(F32).T[:64].astype(BF)
            return c

        lax.fori_loop(0, 8, one, 0)

    def probs(m, c, t, e=None):
        for n, qs in ((256, slice(0, 512)),) if e is None else ((128, slice(0, 256)), (256, slice(256, 512))):
            keys = slice(0, n)
            kv = ks[m, keys, :]
            p = jnp.exp(lax.dot_general(kv, qz[c, qs], NT, preferred_element_type=F32) - lse[c, :, qs])
            if e is not None:
                kp = lax.broadcasted_iota(jnp.int32, p.shape, 0)
                qp = lax.broadcasted_iota(jnp.int32, p.shape, 1) + qs.start
                kpos = (kp // HALF) * 128 + (kp % HALF) + core * 64 + e * HALF
                qpos = (qp // 64) * 128 + (qp % 16) + z * 16
                p = jnp.where(kpos <= qpos, p, 0.0)
            dp = lax.dot_general(kv, dz[c, qs], NT, preferred_element_type=F32)
            dbufs[t, keys, qs] = (p * (dp - dlt[c, :, qs])).astype(BF)
            pbufs[t, keys, qs] = p.astype(BF)

    def dot(a, b):
        return jnp.dot(a, b, preferred_element_type=F32)

    def diag_grads(e, m, t):
        top = dot(dbufs[t, :128, :], qz[m]) + dot(pbufs[t, :128, :], dz[m])
        bottom = dot(dbufs[t, 128:, 256:], qz[m, 256:]) + dot(pbufs[t, 128:, 256:], dz[m, 256:])
        dkv[e, pl.ds(m * 8, 4)] = top.reshape(4, HALF, 128)
        dkv[e, pl.ds(m * 8 + 4, 4)] = bottom.reshape(4, HALF, 128)
        dqt[m, :, :256] += dot(kts[m, :, :128], dbufs[t, :128, :256])
        dqt[m, :, 256:] += dot(kts[m], dbufs[t, :, 256:])

    def grads(e, m, c, t):
        ds, p = dbufs[t], pbufs[t]
        dkv[e, pl.ds(m * 8, 8)] += (dot(ds, qz[c]) + dot(p, dz[c])).reshape(8, HALF, 128)
        dqt[c] += dot(kts[m], ds)

    def diagonal(e):
        def one(i, c):
            for t in range(4):
                probs(4 * i + t, 4 * i + t, t, e)
            for t in range(4):
                diag_grads(e, 4 * i + t, t)
            return c

        lax.fori_loop(0, 2, one, 0)

    def following(m, c):
        wrap = c == 7
        return jnp.where(wrap, m + 1, m), jnp.where(wrap, jnp.minimum(m + 2, 7), c + 1)

    def below(e, n, at, beside=None):
        def four(i, at):
            if beside is not None:
                beside(i)
            tiles = [at]
            for t in range(4):
                probs(*tiles[t], t)
                tiles.append(following(*tiles[t]))
            for t in range(4):
                grads(e, *tiles[t], t)
            return tiles[4]

        return lax.fori_loop(0, n, four, at)

    def r_copy(d, s, u):
        return copy(
            rs_tx.at[d, s, u], rs_rx.at[d, s, u], ZR + 16 + (d * 4 + s) * 2 + u, zdev(1) if d == 0 else zdev(7)
        )

    def terms(e, tz, u):
        parts = []
        for i in range(4):
            b = ((u * 2 + i // 2) * 8 + tz) * 2 + i % 2
            parts.append(dkv[e, stored[0, b]][None])
        return jnp.concatenate(parts, axis=0)

    def r_step(s):
        for u in range(2):
            for d in range(2):
                if s == 0 and u != d:
                    continue
                t = terms(1, (z + 4 - s) % NZ if d == 0 else (z + 4 + s) % NZ, u)
                if s > 1 or (s == 1 and u == d):
                    r_copy(d, s - 1, u).wait_recv()
                    t = t + rs_rx[d, s - 1, u].astype(F32)
                rs_tx[d, s, u] = t.astype(BF)
                sends.append(r_copy(d, s, u))
                sends[-1].start()

    def d_copy(i):
        return copy(d_tx.at[i - 1], d_rx.at[i - 1], ZR + i, zdev(i))

    def d_send():
        for i in Z_STEPS[:-1]:
            for u in range(2):
                d_tx[i - 1, u * 4 : u * 4 + 4] = terms(0, (z + i) % NZ, u).astype(BF)
            sends.append(d_copy(i))
            sends[-1].start()

    def x_copy(e, i):
        src = (x + (0, 0, 3, 1)[i]) % NX
        part = finx.at[e, src] if i < 2 else finx.at[e, src, pl.ds((i - 2) * 4, 4)]
        return copy(part, part, XA + e * 4 + i, xdev((1, 3, 1, 3)[i]))

    def to_owners(e, act):
        rows = pl.ds(pl.multiple_of(core * 64 + e * HALF, HALF), HALF)
        for dx in range(NX):
            for h in range(2):
                tx = (x + dx) % NX
                src, dst = finx.at[e, x, tx * 2 + h], kvg.at[x, rows]
                if dx > 0:
                    act(copy(src, dst, KVR + e, dev(tx, z, h, lo, hi)))
                else:
                    mine = own & (hi == h)

                    @pl.when(jnp.logical_not(mine))
                    def _():
                        act(copy(src, dst, KVR + e, dev(tx, z, h, lo, hi)))

                    @pl.when(mine)
                    def _():
                        act(pltpu.make_async_copy(src, dst, rsem.at[KVR + e]))

    def r_end(e):
        if e == 0:
            for i in range(1, NZ):
                d_copy(i).wait_recv()
        for u in range(2):
            part = slice(u * 4, u * 4 + 4)
            t = terms(e, z, u)
            if e == 0:
                for i in range(1, NZ):
                    t = t + d_rx[i - 1, part].astype(F32)
            else:
                for d in range(2):
                    r_copy(d, 3, u).wait_recv()
                    t = t + rs_rx[d, 3, u].astype(F32)
            finx[e, x, part] = t.astype(BF)
        for i in range(2):
            sends.append(x_copy(e, i))
            sends[-1].start()
        to_owners(e, start)

    def x_forward(e):
        for i in range(2):
            x_copy(e, i).wait_recv()
            sends.append(x_copy(e, 2 + i))
            sends[-1].start()

    def turn_hidden(i):
        e, c = i // 4, i % 4
        cols = pl.ds(pl.multiple_of(c * 128, 128), 128)
        part = hid_buf[:, pl.ds(pl.multiple_of(e * HALF, HALF), HALF), cols].reshape(8 * HALF, 128)
        hid_t[e, cols, :] = part.astype(F32).T.astype(BF)

    def place_q(blk):
        for j in range(4):
            t = (dqt[blk, :, j * 128 : (j + 1) * 128] * 0.125).T
            for o in range(2):
                dqs[blk * 8 + j * 2 + o] = jnp.concatenate(
                    [t[o * 64 + h * 16 : o * 64 + h * 16 + 16] for h in range(4)], axis=1
                )

    z_end(0)
    sort_kv(0)
    to_groups(2, start)
    diagonal(0)
    z_step(1, 2)
    at = below(0, 2, (0, 1))
    z_step(1, 3)
    below(0, 5, at)

    d_send()
    z_end(1)
    sort_kv(1)
    diagonal(1)
    arrived(hid_buf, HID)
    turn_hidden(7)

    def beside(i):
        turn_hidden(i)
        place_q(jnp.maximum(i - 1, 0))

    below(1, 7, (0, 1), beside)
    r_step(0)
    r_end(0)

    for blk in (6, 7):
        place_q(blk)
    r_step(1)

    def give_q(i, c):
        for j in range(4):
            k = i * 4 + j
            dqs_tx[k] = dqs[stored[0, k * 2 + core]]
        return c

    lax.fori_loop(0, 8, give_q, 0)
    sends.append(copy(dqs_tx, dqs_rx, DQS, sib))
    sends[-1].start()
    x_forward(0)
    r_step(2)
    arrived(dqs_rx, DQS)

    def add_q(i, c):
        for j in range(4):
            k = i * 4 + j
            dq_tx[k] = (dqs[stored[0, k * 2 + 1 - core]] + dqs_rx[k]).astype(BF)
        return c

    lax.fori_loop(0, 8, add_q, 0)
    rows, cols = pl.ds(pl.multiple_of(z * 16, 16), 16), pl.ds(pl.multiple_of(x * 256, 256), 256)

    def q_return(i):
        tx, tz = (x + i // NZ) % NX, (z + i) % NZ
        return copy(dq_tx.at[tx * 8 + tz], dq_out.at[rows, cols], DQ, dev(tx, tz, 1 - core, lo, hi))

    def return_q(i, c):
        for j in Z_STEPS:
            q_return(i * NZ + j).start()
        return c

    lax.fori_loop(0, NX, return_q, 0)

    r_step(3)

    def c_copy(i):
        g = (x + i) % NX
        return copy(wpart.at[1 - core, g], c_rx.at[g], CX + i, sib)

    def grad_w(e, i):
        g = (x + i) % NX
        r = dot(hid_t[e], finx[e, g].reshape(8 * HALF, 128)).reshape(32, 2, 8, 128)
        for c in range(2):
            part = r[:, c].reshape(256, 128)
            wpart[c, g] = part if e == 0 else wpart[c, g] + part
        if e == 1:
            sends.append(c_copy(i))
            sends[-1].start()

    for i in range(2):
        x_copy(0, 2 + i).wait_recv()
    for i in range(4):
        grad_w(0, i)
    r_end(1)

    grad_w(1, 0)
    x_forward(1)
    grad_w(1, 3)
    grad_w(1, 1)
    for i in range(2):
        x_copy(1, 2 + i).wait_recv()
    grad_w(1, 2)
    for i in range(4):
        c_copy(i).wait_recv()

    def w_sum(g):
        return (wpart[core, g] + c_rx[g]).reshape(32, 8, 128)

    for i in range(2):
        w_tx[:, :, i * 128 : (i + 1) * 128] = jnp.concatenate([w_sum(i), w_sum(2 + i)], axis=1).astype(BF)

    def w_copy(i):
        tx, tz = (x + i // NZ) % NX, (z + i) % NZ
        return copy(w_tx.at[tx * 8 + tz], w_rx.at[z * 4 + hi * 2 + lo], WR, w_to(i))

    def send_w(i, c):
        for j in Z_STEPS:
            w_copy(i * NZ + j).start()
        return c

    @pl.when(jnp.logical_not(stays))
    def _():
        w_copy(0).start()

    @pl.when(stays)
    def _():
        pltpu.make_async_copy(w_tx.at[x * 8 + z], w_rx.at[z * 4 + hi * 2 + lo], rsem.at[WR]).start()

    for i in Z_STEPS[:-1]:
        w_copy(i).start()
    lax.fori_loop(1, NX, send_w, 0)

    for e in range(2):
        arrived(kvg.at[pl.ds(0, 2)], KVR + e)

    kv_grad = jnp.concatenate([kvg[g, :, :64] for g in range(4)] + [kvg[g, :, 64:] for g in range(4)], axis=1)
    for i in range(4):
        in_out[:, i * 512 : (i + 1) * 512] = lax.dot_general(
            kv_grad, w_all[i], NT, preferred_element_type=F32
        ).astype(BF)

    for i, buf in enumerate(bufs):
        copy(buf.at[got], buf.at[got], Q + i, sib).wait_send()
    copy(dq_tx, dq_tx, DQ, sib).wait_send()
    arrived(dq_tx, DQ)
    for c in sends:
        c.wait_send()

    def sent(c):
        if c.is_remote:
            c.wait_send()

    for i in range(3):
        to_groups(i, sent)
    for e in range(2):
        to_owners(e, sent)

    arrived(w_rx, WR)

    def add_w(i, t):
        return t + w_rx[i].astype(F32)

    total = lax.fori_loop(0, 32, add_w, jnp.zeros((16, 256), F32))
    groups = [total[r : r + 8, c : c + 128] for r in (0, 8) for c in (0, 128)]
    wg_out[...] = jnp.concatenate([g[:, :64] for g in groups] + [g[:, 64:] for g in groups], axis=1)

    @pl.when(stays)
    def _():
        part = w_tx.at[pl.ds(0, 31)]
        copy(part, part, WR, sib).wait_send()

    @pl.when(jnp.logical_not(stays))
    def _():
        copy(w_tx, w_tx, WR, sib).wait_send()


def backward(hid, w, q, do, ao, ls, order):
    v = pltpu.VMEM
    return pl.pallas_call(
        backward_kernel,
        name="backward",
        out_shape=(
            jax.ShapeDtypeStruct((128, 1024), BF),
            jax.ShapeDtypeStruct((128, 2048), BF),
            jax.ShapeDtypeStruct((8, 512), F32),
        ),
        in_specs=[VMEM] * 7,
        out_specs=[VMEM] * 3,
        scratch_shapes=[
            v((4, 8, 1, 128), F32),
            v((1, 64), jnp.int32),
            v((1, 64), jnp.int32),
            v((64, 128), jnp.int32),
            pltpu.SMEM((1, 64), jnp.int32),
            pltpu.SMEM((64, 128), jnp.int32),
            v((4, 512, 512), BF),
            v((128, 512), F32),
            v((4, 128, 128), BF),
            v((64, 16, 256), BF),
            v((64, 16, 256), BF),
            v((64, 1, 128), F32),
            v((64, HALF, 128), BF),
            v((64, HALF, 128), BF),
            v((8, 64, 512), BF),
            v((8, 512, 128), BF),
            v((8, 512, 128), BF),
            v((8, 8 * HALF, 128), BF),
            v((8, 64, 8 * HALF), BF),
            v((8, 1, 512), F32),
            v((8, 1, 512), F32),
            v((8, 64, 512), F32),
            v((2, 64, HALF, 128), F32),
            v((4, 8 * HALF, 512), BF),
            v((4, 8 * HALF, 512), BF),
            v((64, 16, 256), F32),
            v((32, 16, 256), F32),
            v((32, 16, 256), F32),
            v((32, 16, 256), BF),
            v((7, 8, HALF, 128), BF),
            v((7, 8, HALF, 128), BF),
            v((2, 4, 2, 4, HALF, 128), BF),
            v((2, 4, 2, 4, HALF, 128), BF),
            v((2, 4, 8, HALF, 128), BF),
            v((4, 128, 128), BF),
            v((2, 512, 8 * HALF), BF),
            v((2, 4, 256, 128), F32),
            v((4, 256, 128), F32),
            v((32, 16, 256), BF),
            v((32, 16, 256), BF),
            pltpu.SemaphoreType.DMA((N_SEMS + 1,)),
            pltpu.SemaphoreType.DMA((N_SEMS,)),
        ],
        compiler_params=pltpu.CompilerParams(
            collective_id=0, has_side_effects=True, vmem_limit_bytes=56 * 2**20
        ),
    )(hid, w, q, do, ao, ls, order)


def shards(hidden, queries, attn_out, grad_out, log_sums, block_order, w_kv):
    dq_out, in_out, wg = backward(hidden[0], w_kv, queries[0], grad_out[0], attn_out[0], log_sums[0], block_order)
    return dq_out[None], in_out[None], wg


def solution(mesh):
    return jax.shard_map(
        shards,
        mesh=mesh,
        in_specs=(
            P("fsdp", "ctx", None),
            P("fsdp", "ctx", None),
            P("fsdp", "ctx", None),
            P("fsdp", "ctx", None),
            P("fsdp", None, "ctx"),
            P("fsdp", None),
            P("fsdp", None),
        ),
        out_specs=(P("fsdp", "ctx", None), P("fsdp", "ctx", None), P(("fsdp", "ctx"), None)),
        check_vma=False,
    )
```

```python
import functools

import jax
import jax.numpy as jnp
from jax import lax
from jax.experimental import pallas as pl
from jax.experimental.pallas import tpu as pltpu
from jax.sharding import PartitionSpec as P

BF, F32 = jnp.bfloat16, jnp.float32
NT = (((1,), (1,)), ((), ()))
TN = (((0,), (0,)), ((), ()))
MESH = pl.DeviceIdType.MESH
Q_HEADS, KV_HEADS, HEAD_DIM = 16, 4, 64
NX, NZ = 4, 8
Z_STEPS = (4, 1, 7, 3, 5, 2, 6, 0)
VMEM = pl.BlockSpec(memory_space=pltpu.VMEM)


def place():
    f, c = lax.axis_index("fsdp"), lax.axis_index("ctx")
    return c // 16, (c // 2) % 8, c % 2, f // 2, f % 2


def dev(x, z, hi, lo, core):
    return {"fsdp": lo * 2 + core, "ctx": (x * 8 + z) * 2 + hi}


def rcopy(src, dst, send, recv, to):
    return pltpu.make_async_remote_copy(
        src_ref=src, dst_ref=dst, send_sem=send, recv_sem=recv, device_id=to, device_id_type=MESH
    )


def greet(to):
    pl.semaphore_signal(pltpu.get_barrier_semaphore(), inc=1, device_id=to, device_id_type=MESH)

META, W, WF, Q, QF, KV, HID, ZG, ZR, DQS, DQ, KVR, XA, CX, WR = (
    0, 98, 103, 6, 9, 12, 16, 17, 49, 81, 82, 83, 85, 93, 97
)
N_SEMS = 107
HALF = 32


def backward_kernel(
    hid, w, q, do, ao, ls, mine_order,
    dq_out, in_out, wg_out,
    stat, sib_order, stored_vm, sorted_vm, stored, sorted_, w_all, acc, kvs, q_buf, do_buf, stat_buf, kv_buf0, kv_buf1, hid_buf,
    qz, dz, ks, kts, lse, dlt, dqt, dkv, pbufs, dbufs,
    dqs, dqs_tx, dqs_rx, dq_tx, d_tx, d_rx, rs_tx, rs_rx, finx, kvg, hid_t, wpart, c_rx, w_tx, w_rx,
    ssem, rsem,
):
    x, z, hi, lo, core = place()
    f = lo * 2 + core
    sib = dev(x, z, hi, lo, 1 - core)
    near = dev(x, z, hi, 1 - lo, core)
    far = dev(x, z, 1 - hi, 1 - lo, core)
    own = hi == core

    def xdev(i):
        return dev((x + i) % NX, z, hi, lo, core)

    def zdev(i):
        return dev(x, (z + i) % NZ, hi, lo, core)

    def copy(src, dst, sem, to):
        return rcopy(src, dst, ssem.at[sem], rsem.at[sem], to)

    def arrived(ref, sem):
        rcopy(ref, ref, ssem.at[sem], rsem.at[sem], sib).wait_recv()

    for to in [sib, near, far, xdev(1), xdev(3)] + [zdev(i) for i in range(1, NZ)]:
        greet(to)

    def greet_q(i, c):
        for j in range(4):
            greet(dev((x + i // 2) % NX, (z + i * 4 + j) % NZ, 1 - core, lo, hi))
        return c

    lax.fori_loop(0, 8, greet_q, 0)

    def greet_kv(i, c):
        dx, h = i // 2, i % 2

        @pl.when(jnp.logical_not((dx == 0) & own & (h == hi)))
        def _():
            greet(dev((x + dx) % NX, z, h, lo, hi))

        return c

    lax.fori_loop(0, 8, greet_kv, 0)

    stays = own & (x // 2 == lo) & (x % 2 == core)

    def w_from(i):
        return dev(f, (z + i) % NZ, (hi + i // 16) % 2, (lo + i // 8) % 2, hi)

    def w_to(i):
        return dev((x + i // NZ) % NX, (z + i) % NZ, core, x // 2, x % 2)

    def greet_w(i, c):
        for j in range(4):
            greet(w_from(i * 4 + j))
        return c

    @pl.when(jnp.logical_not(stays))
    def _():
        greet(w_from(0))

    for i in range(1, 4):
        greet(w_from(i))
    lax.fori_loop(1, 8, greet_w, 0)
    pl.semaphore_wait(
        pltpu.get_barrier_semaphore(), 12 + 32 + 8 + 32 - own.astype(jnp.int32) - stays.astype(jnp.int32)
    )

    w_own = pltpu.make_async_copy(w, w_all.at[f], ssem.at[N_SEMS])
    w_own.start()
    quarter = w.shape[0] // 4

    def w_rows(i):
        return pl.ds(i * quarter, quarter)

    sends = [
        copy(w.at[w_rows(i)], w_all.at[f, w_rows(i)], W + i, far if i % 2 else near) for i in range(4)
    ]
    sends.append(copy(w, w_all.at[f], W + 4, sib))
    sends.append(copy(mine_order, sib_order, META, sib))
    for c in sends:
        c.start()

    slot = hi * 32 + x * 8 + z

    def q_copies(i):
        tx, tz = (x + i // NZ) % NX, (z + i) % NZ
        to = dev(tx, tz, core, lo, 1 - hi)
        rows, cols = pl.ds(pl.multiple_of(tz * 16, 16), 16), pl.ds(pl.multiple_of(tx * 256, 256), 256)
        return (
            copy(q.at[rows, cols], q_buf.at[slot], Q, to),
            copy(do.at[rows, cols], do_buf.at[slot], Q + 1, to),
        )

    def send_q(i, c):
        for j in Z_STEPS:
            for one in q_copies(i * NZ + j):
                one.start()
        return c

    lax.fori_loop(0, NX, send_q, 0)

    def project(chunk):
        cols = pl.ds(pl.multiple_of(chunk * 512, 512), 512)
        return jnp.dot(hid[:, cols], w_all[chunk], preferred_element_type=F32)

    w_own.wait()
    acc[...] = project(f)
    arrived(w_all.at[0], W + 4)
    acc[...] += project(lo * 2 + 1 - core)
    other, last = (1 - lo) * 2 + core, (1 - lo) * 2 + 1 - core
    for i in range(4):
        part = w_all.at[other, w_rows(i)]
        arrived(part, W + i)
        sends.append(copy(part, part, WF + i, sib))
        sends[-1].start()
    acc[...] += project(other)
    for i in range(4):
        arrived(w_all.at[last, w_rows(i)], WF + i)
    key_vals = (acc[...] + project(last)).astype(BF)
    for g in range(KV_HEADS):
        kvs[g] = jnp.concatenate(
            [key_vals[:, g * 64 : g * 64 + 64], key_vals[:, 256 + g * 64 : 320 + g * 64]], axis=1
        )

    kv_buf = (kv_buf0, kv_buf1)

    def to_group(dx, j, which):
        tx = (x + dx) % NX
        to = dev(tx, z, core, lo, j)
        mine = x * 2 + hi
        if which < 2:
            rows = pl.ds(j * 64 + which * HALF, HALF)
            return (kvs.at[tx, rows], kv_buf[which].at[z * 8 + mine], KV + which * 2 + x // 2), to
        rows, cols = pl.ds(j * 64, 64), pl.ds(pl.multiple_of(tx * 512, 512), 512)
        return (hid.at[rows, cols], hid_buf.at[mine], HID), to

    def to_groups(which, act):
        for dx in range(NX):
            for j in range(2):
                piece, to = to_group(dx, j, which)
                if dx > 0:
                    act(copy(*piece, to))
                else:
                    mine = own & (core == j)

                    @pl.when(jnp.logical_not(mine))
                    def _():
                        act(copy(*piece, to))

                    @pl.when(mine)
                    def _():
                        src, dst, sem = piece
                        act(pltpu.make_async_copy(src, dst, rsem.at[sem]))

    def start(c):
        c.start()

    to_groups(0, start)
    to_groups(1, start)

    prod = do[...].astype(F32) * ao[...].astype(F32)
    heads = lax.broadcasted_iota(jnp.int32, (Q_HEADS, Q_HEADS * HEAD_DIM), 0)
    pick = (lax.broadcasted_iota(jnp.int32, heads.shape, 1) // HEAD_DIM == heads).astype(F32).astype(BF)
    delta = jnp.zeros((Q_HEADS, 128), F32)
    for _ in range(3):
        term = prod.astype(BF)
        delta = delta + lax.dot_general(pick, term, NT, preferred_element_type=F32)
        prod = prod - term.astype(F32)
    turned = [[t] + [pltpu.roll(t, 16 * s, 1) for s in range(1, 8)] for t in (ls[...], delta)]
    head_of = lax.broadcasted_iota(jnp.int32, (Q_HEADS, 128), 0) % 4
    lanes_of = lax.broadcasted_iota(jnp.int32, (Q_HEADS, 128), 1) // 16
    for tz in range(NZ):
        row = jnp.zeros((Q_HEADS, 128), F32)
        for k in range(2):
            for h in range(4):
                row = jnp.where(
                    (head_of == h) & (lanes_of == h + 4 * k), turned[k][(h + 4 * k - tz) % 8], row
                )
        row = row + pltpu.roll(row, Q_HEADS - 1, 0)
        row = row + pltpu.roll(row, Q_HEADS - 2, 0)
        for g in range(4):
            stat[g, tz] = row[4 * g : 4 * g + 1, :]

    def send_stat(i, c):
        for j in Z_STEPS:
            tx, tz = (x + i) % NX, (z + j) % NZ
            copy(stat.at[tx, tz], stat_buf.at[slot], Q + 2, dev(tx, tz, core, lo, 1 - hi)).start()
        return c

    lax.fori_loop(0, NX, send_stat, 0)


    def z_part(src_z, u):
        return pl.ds(pl.multiple_of(src_z * 8 + u * 4, 4), 4)

    def z_copy(e, d, s, u):
        part = kv_buf[e].at[z_part((z + 8 - s) % NZ if d == 0 else (z + s) % NZ, u)]
        return copy(part, part, ZG + e * 16 + (d * 4 + s) * 2 + u, zdev(1) if d == 0 else zdev(7))

    def z_step(e, s):
        for u in range(2):
            if s == 0:
                arrived(kv_buf[e].at[pl.ds(0, 4)], KV + e * 2 + u)
            for d in range(2):
                if s == 3 and u != d:
                    continue
                if s:
                    z_copy(e, d, s - 1, u).wait_recv()
                sends.append(z_copy(e, d, s, u))
                sends[-1].start()

    def z_end(e):
        for d, s, u in ((0, 2, 1), (1, 2, 0), (0, 3, 0), (1, 3, 1)):
            z_copy(e, d, s, u).wait_recv()

    z_step(0, 0)
    z_step(0, 1)
    z_step(1, 0)
    z_step(0, 2)
    z_step(0, 3)

    got = pl.ds(pl.multiple_of((1 - core) * 32, 32), 32)
    theirs = pl.ds(pl.multiple_of(core * 32, 32), 32)
    bufs = (q_buf, do_buf, stat_buf)
    for i, buf in enumerate(bufs):
        arrived(buf.at[got], Q + i)
        sends.append(copy(buf.at[got], buf.at[got], QF + i, sib))
        sends[-1].start()

    arrived(sib_order, META)
    there = jnp.where(own, mine_order[...], sib_order[...])
    ids = lax.broadcasted_iota(jnp.int32, (64, 64), 1)
    back = jnp.max(jnp.where(there == lax.broadcasted_iota(jnp.int32, (64, 64), 0), ids, 0), axis=1, keepdims=True)
    stored_vm[...] = there
    sorted_vm[...] = jnp.broadcast_to(back, (64, 128))
    for vm, sm in ((stored_vm, stored), (sorted_vm, sorted_)):
        c = pltpu.make_async_copy(vm, sm, ssem.at[N_SEMS])
        c.start()
        c.wait()

    for i, buf in enumerate(bufs):
        arrived(buf.at[theirs], QF + i)

    low = lax.broadcasted_iota(jnp.int32, (16, 128), 1) < 64
    low1 = lax.broadcasted_iota(jnp.int32, (1, 128), 1) < 64

    def sort_q(blk, c):
        stats = []
        for off in range(8):
            b = sorted_[blk * 8 + off, 0]
            s = (b % 2) * 32 + b // 2
            for hp in range(2):
                qq = q_buf[s, :, hp * 128 : (hp + 1) * 128].astype(F32) * 0.125
                dd = do_buf[s, :, hp * 128 : (hp + 1) * 128].astype(F32)
                for ho in range(2):
                    rows = slice(off * 64 + hp * 32 + ho * 16, off * 64 + hp * 32 + ho * 16 + 16)
                    qh = qq if ho == 0 else pltpu.roll(qq, 64, 1)
                    dh = dd if ho == 1 else pltpu.roll(dd, 64, 1)
                    qz[blk, rows, :] = jnp.where(low, qh, 0.0).astype(BF)
                    dz[blk, rows, :] = jnp.where(low, 0.0, dh).astype(BF)
            stats.append(stat_buf[s])
        for j in range(4):
            a, b = stats[2 * j], stats[2 * j + 1]
            lse[blk, :, j * 128 : (j + 1) * 128] = jnp.where(low1, a, pltpu.roll(b, 64, 1))
            dlt[blk, :, j * 128 : (j + 1) * 128] = jnp.where(low1, pltpu.roll(a, 64, 1), b)
        dqt[blk] = jnp.zeros((64, 512), F32)
        return c

    lax.fori_loop(0, 8, sort_q, 0)
    z_step(1, 1)

    def sort_kv(e):
        def one(blk, c):
            for off in range(8):
                b = sorted_[blk * 8 + off, 0]
                ks[blk, off * HALF : (off + 1) * HALF, :] = kv_buf[e][((b // 2) % 8) * 8 + (b // 16) * 2 + b % 2]
            kts[blk] = ks[blk].astype(F32).T[:64].astype(BF)
            return c

        lax.fori_loop(0, 8, one, 0)

    def probs(m, c, t, e=None):
        for n, qs in ((256, slice(0, 512)),) if e is None else ((128, slice(0, 256)), (256, slice(256, 512))):
            keys = slice(0, n)
            kv = ks[m, keys, :]
            p = jnp.exp(lax.dot_general(kv, qz[c, qs], NT, preferred_element_type=F32) - lse[c, :, qs])
            if e is not None:
                kp = lax.broadcasted_iota(jnp.int32, p.shape, 0)
                qp = lax.broadcasted_iota(jnp.int32, p.shape, 1) + qs.start
                kpos = (kp // HALF) * 128 + (kp % HALF) + core * 64 + e * HALF
                qpos = (qp // 64) * 128 + (qp % 16) + z * 16
                p = jnp.where(kpos <= qpos, p, 0.0)
            dp = lax.dot_general(kv, dz[c, qs], NT, preferred_element_type=F32)
            dbufs[t, keys, qs] = (p * (dp - dlt[c, :, qs])).astype(BF)
            pbufs[t, keys, qs] = p.astype(BF)

    def dot(a, b):
        return jnp.dot(a, b, preferred_element_type=F32)

    def diag_grads(e, m, t):
        top = dot(dbufs[t, :128, :], qz[m]) + dot(pbufs[t, :128, :], dz[m])
        bottom = dot(dbufs[t, 128:, 256:], qz[m, 256:]) + dot(pbufs[t, 128:, 256:], dz[m, 256:])
        dkv[e, pl.ds(m * 8, 4)] = top.reshape(4, HALF, 128)
        dkv[e, pl.ds(m * 8 + 4, 4)] = bottom.reshape(4, HALF, 128)
        dqt[m, :, :256] += dot(kts[m, :, :128], dbufs[t, :128, :256])
        dqt[m, :, 256:] += dot(kts[m], dbufs[t, :, 256:])

    def grads(e, m, c, t):
        ds, p = dbufs[t], pbufs[t]
        dkv[e, pl.ds(m * 8, 8)] += (dot(ds, qz[c]) + dot(p, dz[c])).reshape(8, HALF, 128)
        dqt[c] += dot(kts[m], ds)

    def diagonal(e):
        def one(i, c):
            for t in range(4):
                probs(4 * i + t, 4 * i + t, t, e)
            for t in range(4):
                diag_grads(e, 4 * i + t, t)
            return c

        lax.fori_loop(0, 2, one, 0)

    def following(m, c):
        wrap = c == 7
        return jnp.where(wrap, m + 1, m), jnp.where(wrap, jnp.minimum(m + 2, 7), c + 1)

    def below(e, n, at, beside=None):
        def four(i, at):
            if beside is not None:
                beside(i)
            tiles = [at]
            for t in range(4):
                probs(*tiles[t], t)
                tiles.append(following(*tiles[t]))
            for t in range(4):
                grads(e, *tiles[t], t)
            return tiles[4]

        return lax.fori_loop(0, n, four, at)

    def r_copy(d, s, u):
        return copy(
            rs_tx.at[d, s, u], rs_rx.at[d, s, u], ZR + 16 + (d * 4 + s) * 2 + u, zdev(1) if d == 0 else zdev(7)
        )

    def terms(e, tz, u):
        parts = []
        for i in range(4):
            b = ((u * 2 + i // 2) * 8 + tz) * 2 + i % 2
            parts.append(dkv[e, stored[0, b]][None])
        return jnp.concatenate(parts, axis=0)

    def r_step(s):
        for u in range(2):
            for d in range(2):
                if s == 0 and u != d:
                    continue
                t = terms(1, (z + 4 - s) % NZ if d == 0 else (z + 4 + s) % NZ, u)
                if s > 1 or (s == 1 and u == d):
                    r_copy(d, s - 1, u).wait_recv()
                    t = t + rs_rx[d, s - 1, u].astype(F32)
                rs_tx[d, s, u] = t.astype(BF)
                sends.append(r_copy(d, s, u))
                sends[-1].start()

    def d_copy(i):
        return copy(d_tx.at[i - 1], d_rx.at[i - 1], ZR + i, zdev(i))

    def d_send():
        for i in Z_STEPS[:-1]:
            for u in range(2):
                d_tx[i - 1, u * 4 : u * 4 + 4] = terms(0, (z + i) % NZ, u).astype(BF)
            sends.append(d_copy(i))
            sends[-1].start()

    def x_copy(e, i):
        src = (x + (0, 0, 3, 1)[i]) % NX
        part = finx.at[e, src] if i < 2 else finx.at[e, src, pl.ds((i - 2) * 4, 4)]
        return copy(part, part, XA + e * 4 + i, xdev((1, 3, 1, 3)[i]))

    def to_owners(e, act):
        rows = pl.ds(pl.multiple_of(core * 64 + e * HALF, HALF), HALF)
        for dx in range(NX):
            for h in range(2):
                tx = (x + dx) % NX
                src, dst = finx.at[e, x, tx * 2 + h], kvg.at[x, rows]
                if dx > 0:
                    act(copy(src, dst, KVR + e, dev(tx, z, h, lo, hi)))
                else:
                    mine = own & (hi == h)

                    @pl.when(jnp.logical_not(mine))
                    def _():
                        act(copy(src, dst, KVR + e, dev(tx, z, h, lo, hi)))

                    @pl.when(mine)
                    def _():
                        act(pltpu.make_async_copy(src, dst, rsem.at[KVR + e]))

    def r_end(e):
        if e == 0:
            for i in range(1, NZ):
                d_copy(i).wait_recv()
        for u in range(2):
            part = slice(u * 4, u * 4 + 4)
            t = terms(e, z, u)
            if e == 0:
                for i in range(1, NZ):
                    t = t + d_rx[i - 1, part].astype(F32)
            else:
                for d in range(2):
                    r_copy(d, 3, u).wait_recv()
                    t = t + rs_rx[d, 3, u].astype(F32)
            finx[e, x, part] = t.astype(BF)
        for i in range(2):
            sends.append(x_copy(e, i))
            sends[-1].start()
        to_owners(e, start)

    def x_forward(e):
        for i in range(2):
            x_copy(e, i).wait_recv()
            sends.append(x_copy(e, 2 + i))
            sends[-1].start()

    def turn_hidden(i):
        e, c = i // 4, i % 4
        cols = pl.ds(pl.multiple_of(c * 128, 128), 128)
        part = hid_buf[:, pl.ds(pl.multiple_of(e * HALF, HALF), HALF), cols].reshape(8 * HALF, 128)
        hid_t[e, cols, :] = part.astype(F32).T.astype(BF)

    def place_q(blk):
        for j in range(4):
            t = (dqt[blk, :, j * 128 : (j + 1) * 128] * 0.125).T
            for o in range(2):
                dqs[blk * 8 + j * 2 + o] = jnp.concatenate(
                    [t[o * 64 + h * 16 : o * 64 + h * 16 + 16] for h in range(4)], axis=1
                )

    z_end(0)
    sort_kv(0)
    to_groups(2, start)
    diagonal(0)
    z_step(1, 2)
    at = below(0, 2, (0, 1))
    z_step(1, 3)
    below(0, 5, at)

    d_send()
    z_end(1)
    sort_kv(1)
    diagonal(1)
    arrived(hid_buf, HID)
    turn_hidden(7)

    def beside(i):
        turn_hidden(i)
        place_q(jnp.maximum(i - 1, 0))

    below(1, 7, (0, 1), beside)
    r_step(0)

    for blk in (6, 7):
        place_q(blk)

    def give_q(i, c):
        for j in range(4):
            k = i * 4 + j
            dqs_tx[k] = dqs[stored[0, k * 2 + core]]
        return c

    lax.fori_loop(0, 8, give_q, 0)
    sends.append(copy(dqs_tx, dqs_rx, DQS, sib))
    sends[-1].start()
    r_step(1)
    r_end(0)
    r_step(2)
    x_forward(0)
    arrived(dqs_rx, DQS)

    def add_q(i, c):
        for j in range(4):
            k = i * 4 + j
            dq_tx[k] = (dqs[stored[0, k * 2 + 1 - core]] + dqs_rx[k]).astype(BF)
        return c

    lax.fori_loop(0, 8, add_q, 0)
    rows, cols = pl.ds(pl.multiple_of(z * 16, 16), 16), pl.ds(pl.multiple_of(x * 256, 256), 256)

    def q_return(i):
        tx, tz = (x + i // NZ) % NX, (z + i) % NZ
        return copy(dq_tx.at[tx * 8 + tz], dq_out.at[rows, cols], DQ, dev(tx, tz, 1 - core, lo, hi))

    def return_q(i, c):
        for j in Z_STEPS:
            q_return(i * NZ + j).start()
        return c

    lax.fori_loop(0, NX, return_q, 0)

    r_step(3)

    def c_copy(i):
        g = (x + i) % NX
        return copy(wpart.at[1 - core, g], c_rx.at[g], CX + i, sib)

    def grad_w(e, i):
        g = (x + i) % NX
        r = dot(hid_t[e], finx[e, g].reshape(8 * HALF, 128)).reshape(32, 2, 8, 128)
        for c in range(2):
            part = r[:, c].reshape(256, 128)
            wpart[c, g] = part if e == 0 else wpart[c, g] + part
        if e == 1:
            sends.append(c_copy(i))
            sends[-1].start()

    for i in range(2):
        x_copy(0, 2 + i).wait_recv()
    for i in range(4):
        grad_w(0, i)
    r_end(1)

    grad_w(1, 0)
    x_forward(1)
    grad_w(1, 3)
    grad_w(1, 1)
    for i in range(2):
        x_copy(1, 2 + i).wait_recv()
    grad_w(1, 2)
    for i in range(4):
        c_copy(i).wait_recv()

    def w_sum(g):
        return (wpart[core, g] + c_rx[g]).reshape(32, 8, 128)

    for i in range(2):
        w_tx[:, :, i * 128 : (i + 1) * 128] = jnp.concatenate([w_sum(i), w_sum(2 + i)], axis=1).astype(BF)

    def w_copy(i):
        tx, tz = (x + i // NZ) % NX, (z + i) % NZ
        return copy(w_tx.at[tx * 8 + tz], w_rx.at[z * 4 + hi * 2 + lo], WR, w_to(i))

    def send_w(i, c):
        for j in Z_STEPS:
            w_copy(i * NZ + j).start()
        return c

    @pl.when(jnp.logical_not(stays))
    def _():
        w_copy(0).start()

    @pl.when(stays)
    def _():
        pltpu.make_async_copy(w_tx.at[x * 8 + z], w_rx.at[z * 4 + hi * 2 + lo], rsem.at[WR]).start()

    for i in Z_STEPS[:-1]:
        w_copy(i).start()
    lax.fori_loop(1, NX, send_w, 0)

    for e in range(2):
        arrived(kvg.at[pl.ds(0, 2)], KVR + e)

    kv_grad = jnp.concatenate([kvg[g, :, :64] for g in range(4)] + [kvg[g, :, 64:] for g in range(4)], axis=1)
    for i in range(4):
        in_out[:, i * 512 : (i + 1) * 512] = lax.dot_general(
            kv_grad, w_all[i], NT, preferred_element_type=F32
        ).astype(BF)

    for i, buf in enumerate(bufs):
        copy(buf.at[got], buf.at[got], Q + i, sib).wait_send()
    copy(dq_tx, dq_tx, DQ, sib).wait_send()
    arrived(dq_tx, DQ)
    for c in sends:
        c.wait_send()

    def sent(c):
        if c.is_remote:
            c.wait_send()

    for i in range(3):
        to_groups(i, sent)
    for e in range(2):
        to_owners(e, sent)

    arrived(w_rx, WR)

    def add_w(i, t):
        return t + w_rx[i].astype(F32)

    total = lax.fori_loop(0, 32, add_w, jnp.zeros((16, 256), F32))
    groups = [total[r : r + 8, c : c + 128] for r in (0, 8) for c in (0, 128)]
    wg_out[...] = jnp.concatenate([g[:, :64] for g in groups] + [g[:, 64:] for g in groups], axis=1)

    @pl.when(stays)
    def _():
        part = w_tx.at[pl.ds(0, 31)]
        copy(part, part, WR, sib).wait_send()

    @pl.when(jnp.logical_not(stays))
    def _():
        copy(w_tx, w_tx, WR, sib).wait_send()


def backward(hid, w, q, do, ao, ls, order):
    v = pltpu.VMEM
    return pl.pallas_call(
        backward_kernel,
        name="backward",
        out_shape=(
            jax.ShapeDtypeStruct((128, 1024), BF),
            jax.ShapeDtypeStruct((128, 2048), BF),
            jax.ShapeDtypeStruct((8, 512), F32),
        ),
        in_specs=[VMEM] * 7,
        out_specs=[VMEM] * 3,
        scratch_shapes=[
            v((4, 8, 1, 128), F32),
            v((1, 64), jnp.int32),
            v((1, 64), jnp.int32),
            v((64, 128), jnp.int32),
            pltpu.SMEM((1, 64), jnp.int32),
            pltpu.SMEM((64, 128), jnp.int32),
            v((4, 512, 512), BF),
            v((128, 512), F32),
            v((4, 128, 128), BF),
            v((64, 16, 256), BF),
            v((64, 16, 256), BF),
            v((64, 1, 128), F32),
            v((64, HALF, 128), BF),
            v((64, HALF, 128), BF),
            v((8, 64, 512), BF),
            v((8, 512, 128), BF),
            v((8, 512, 128), BF),
            v((8, 8 * HALF, 128), BF),
            v((8, 64, 8 * HALF), BF),
            v((8, 1, 512), F32),
            v((8, 1, 512), F32),
            v((8, 64, 512), F32),
            v((2, 64, HALF, 128), F32),
            v((4, 8 * HALF, 512), BF),
            v((4, 8 * HALF, 512), BF),
            v((64, 16, 256), F32),
            v((32, 16, 256), F32),
            v((32, 16, 256), F32),
            v((32, 16, 256), BF),
            v((7, 8, HALF, 128), BF),
            v((7, 8, HALF, 128), BF),
            v((2, 4, 2, 4, HALF, 128), BF),
            v((2, 4, 2, 4, HALF, 128), BF),
            v((2, 4, 8, HALF, 128), BF),
            v((4, 128, 128), BF),
            v((2, 512, 8 * HALF), BF),
            v((2, 4, 256, 128), F32),
            v((4, 256, 128), F32),
            v((32, 16, 256), BF),
            v((32, 16, 256), BF),
            pltpu.SemaphoreType.DMA((N_SEMS + 1,)),
            pltpu.SemaphoreType.DMA((N_SEMS,)),
        ],
        compiler_params=pltpu.CompilerParams(
            collective_id=0, has_side_effects=True, vmem_limit_bytes=56 * 2**20
        ),
    )(hid, w, q, do, ao, ls, order)


def shards(hidden, queries, attn_out, grad_out, log_sums, block_order, w_kv):
    dq_out, in_out, wg = backward(hidden[0], w_kv, queries[0], grad_out[0], attn_out[0], log_sums[0], block_order)
    return dq_out[None], in_out[None], wg


def solution(mesh):
    return jax.shard_map(
        shards,
        mesh=mesh,
        in_specs=(
            P("fsdp", "ctx", None),
            P("fsdp", "ctx", None),
            P("fsdp", "ctx", None),
            P("fsdp", "ctx", None),
            P("fsdp", None, "ctx"),
            P("fsdp", None),
            P("fsdp", None),
        ),
        out_specs=(P("fsdp", "ctx", None), P("fsdp", "ctx", None), P(("fsdp", "ctx"), None)),
        check_vma=False,
    )
```
